32 devices in a mesh: rows: 4 (over y, x), tm: 8 (over z, core).
Axes of the slice: x: 2, y: 2, z: 4, core: 2. Of those that a mesh axis runs over, the one named last changes fastest.
Arguments:
- snapshots: float32 [4096, 2048], P('rows', 'tm'), may hold values from -16 to 16
- right_basis: float32 [2048, 256], P('tm'), may hold values from -0.125 to 0.125
- threshold: float32 [2048], P('tm'), may hold values from 0.3 to 3
Outputs:
- low_rank: float32 [4096, 2048], P('rows', 'tm')
- sparse: float32 [4096, 2048], P('rows', 'tm')
The draws below stay inside these ranges and needn't reach their ends.
All inputs are finite; a program needn't handle non-finite values.
Results may differ from the reference program's by a relative error of at most 0.0003.
Values sent between devices are 32-bit elements; how exact they have to be, the bound alone decides.
No kernel may reach another device: no remote copies, remote signals or barrier semaphores. Data moves between devices by JAX's collectives and lax.ppermute only.
A program may use at most 64 MiB of HBM per device.

```python
import math
import jax
import jax.numpy as jnp
from jax import lax

R = 256
ITERS = 2
UNKNOWNS = 4096
TIMES = 2048


def draw_snapshots(key, part):
    mode_count = 2 * R
    mode_index = jnp.arange(mode_count, dtype=jnp.float32)
    spectrum = jnp.exp(-mode_index * (math.log(4.0) / R))
    energy = jnp.sum(spectrum * spectrum)
    spectrum = spectrum * jnp.sqrt(4.0 * UNKNOWNS * TIMES / energy)
    key_left = jax.random.fold_in(key, 11)
    key_right = jax.random.fold_in(key, 12)
    key_mask = jax.random.fold_in(key, 13)
    key_size = jax.random.fold_in(key, 14)
    key_sign = jax.random.fold_in(key, 15)
    key_noise = jax.random.fold_in(key, 16)
    grid_shape = (UNKNOWNS, TIMES)
    left_factor = jax.random.normal(key_left, (UNKNOWNS, mode_count), jnp.float32) * math.sqrt(1.0 / UNKNOWNS)
    right_factor = jax.random.normal(key_right, (mode_count, TIMES), jnp.float32) * math.sqrt(1.0 / TIMES)
    amplitude = jax.random.uniform(key_size, grid_shape, jnp.float32, 1.0, 4.0)
    noise_part = 0.05 * jax.random.normal(key_noise, grid_shape, jnp.float32)
    mask_hit = jax.random.uniform(key_mask, grid_shape, jnp.float32) < 1.0 / 128.0
    sign_pick = jnp.where(jax.random.uniform(key_sign, grid_shape, jnp.float32) < 0.5, -1.0, 1.0)
    spikes = jnp.where(mask_hit, sign_pick * amplitude, 0.0)
    smooth = jnp.dot(left_factor * spectrum[None, :], right_factor, precision=lax.Precision.HIGHEST)
    return jnp.clip(smooth + spikes + noise_part, -16.0, 16.0).astype(jnp.float32)


def levels(stream_key, shape, cuts, smallest, top_value):
    factor_of, own = 1.0, jax.random.fold_in(stream_key, 6)
    for axis_at, parts in cuts:
        heights = jnp.exp(jax.random.uniform(jax.random.fold_in(own, axis_at), (parts,), jnp.float32, smallest / len(cuts), top_value / len(cuts)))
        factor_of = factor_of * jnp.repeat(heights, shape[axis_at] // parts).reshape([-1 if axis == axis_at else 1 for axis in range(len(shape))])
    return factor_of


def gaussian(own_key, shape, scale, limit, shards=(), held_as=jnp.bfloat16):
    array = scale * jax.random.normal(own_key, shape, jnp.float32)
    if shards:
        array = array * levels(own_key, shape, shards, -0.22, 0.18)
    return jnp.clip(array, -limit, limit).astype(held_as)


def setup_inputs(seed: int = 0) -> dict:
    seeds = jax.random.split(jax.random.key(seed), 4)
    return {
        "snapshots": draw_snapshots(jax.random.fold_in(seeds[3], 71), 0),
        "right_basis": gaussian(seeds[1], (TIMES, R), TIMES ** -0.5, 0.125, ((0, 8),), jnp.float32),
        "threshold": jnp.clip(jnp.exp(math.log(3.0) - 2.3025851 * jax.random.uniform(seeds[2], (TIMES,), jnp.float32) ** levels(seeds[2], (TIMES,), ((0, 8),), -0.2, 0.2)), 0.3, 3.0),
    }


highest = lax.Precision.HIGHEST

def gram_of(matrix):
    return lax.dot_general(matrix.astype(jnp.float32), matrix.astype(jnp.float32), (((0,), (0,)), ((), ())), precision=highest, preferred_element_type=jnp.float32)

def inverse_factor(gram):
    lower = jnp.linalg.cholesky(gram)
    identity_rows = jnp.eye(gram.shape[0], dtype=gram.dtype)
    return lax.linalg.triangular_solve(lower, identity_rows, left_side=True, lower=True)

def times_inverse(matrix, inverse):
    return lax.dot_general(matrix.astype(jnp.float32), inverse.astype(jnp.float32), (((1,), (1,)), ((), ())), precision=highest, preferred_element_type=jnp.float32)

def reference(snapshots, right_basis, threshold):
    sparse = jnp.zeros_like(snapshots)
    basis = right_basis
    low_rank = jnp.zeros_like(snapshots)
    for iteration in range(ITERS):
        residual = snapshots - sparse
        left = jnp.dot(residual.astype(jnp.float32), basis.astype(jnp.float32), precision=highest, preferred_element_type=jnp.float32)
        ortho = times_inverse(left, inverse_factor(gram_of(left)))
        basis = lax.dot_general(residual.astype(jnp.float32), ortho.astype(jnp.float32), (((0,), (0,)), ((), ())), precision=highest, preferred_element_type=jnp.float32)
        low_rank = times_inverse(ortho, basis)
        difference = snapshots - low_rank
        sparse = jnp.sign(difference) * jnp.maximum(jnp.abs(difference) - threshold[None, :], 0.0)
    return (low_rank, sparse)
```

```python
import functools
import jax
import jax.numpy as jnp
from jax import lax
from jax.experimental import pallas as pl
from jax.experimental.pallas import tpu as pltpu
from jax.sharding import PartitionSpec as P

ITERS = 2
CHUNKS = 2

high = lax.Precision.HIGH
highest = lax.Precision.HIGHEST
NN = (((1,), (0,)), ((), ()))
NT = (((1,), (1,)), ((), ()))
TN = (((0,), (0,)), ((), ()))


def mm(a, b, dims, precision=high):
    return lax.dot_general(a, b, dims, precision=precision, preferred_element_type=jnp.float32)


def swap(x, axis, size, bit):
    return lax.ppermute(x, axis, [(i, i ^ bit) for i in range(size)])


def reorder(x, me, blocks):
    rows, cols = x.shape
    cut = x.reshape(CHUNKS, blocks, rows // (CHUNKS * blocks), cols)
    parts = [lax.dynamic_slice_in_dim(cut, p ^ me, 1, 1) for p in range(blocks)]
    return jnp.concatenate(parts, 1).reshape(rows, cols)


def sum_tm(chunks, size):
    bits = [1 << b for b in range(size.bit_length() - 1)]
    chunks = list(chunks)
    for bit in bits[:-1]:
        for i, x in enumerate(chunks):
            half = x.shape[0] // 2
            kept, sent = x[:half], x[half:]
            chunks[i] = kept + swap(sent, "tm", size, bit)
    for i, x in enumerate(chunks):
        chunks[i] = x + swap(x, "tm", size, bits[-1])
    for bit in reversed(bits[:-1]):
        for i, x in enumerate(chunks):
            chunks[i] = jnp.concatenate([x, swap(x, "tm", size, bit)], 0)
    return chunks


def sum_rows(x, size):
    bits = [1 << b for b in range(size.bit_length() - 1)]
    half = x.shape[0] // 2
    a, b = x[:half], x[half:]
    turn = len(bits) // 2
    for bit_a, bit_b in zip(bits, bits[turn:] + bits[:turn]):
        a, b = a + swap(a, "rows", size, bit_a), b + swap(b, "rows", size, bit_b)
    return jnp.concatenate([a, b], 0)


def halves(x):
    top = x.astype(jnp.bfloat16)
    return top, (x - top.astype(jnp.float32)).astype(jnp.bfloat16)


def dot3(a, b):
    a1, a2 = halves(a)
    b1, b2 = halves(b)
    dot = functools.partial(jnp.dot, preferred_element_type=jnp.float32)
    return dot(a1, b1) + (dot(a1, b2) + dot(a2, b1))


def dot6(a, b):
    return jnp.dot(a, b, precision=highest, preferred_element_type=jnp.float32)


def solve_kernel(gram_ref, right_ref, out_ref):
    gram = gram_ref[...]
    n = gram.shape[0]
    eye = (
        lax.broadcasted_iota(jnp.int32, (n, n), 0) == lax.broadcasted_iota(jnp.int32, (n, n), 1)
    ).astype(jnp.float32)
    on_diag = gram * eye
    down = lax.rsqrt(jnp.sum(on_diag, 1, keepdims=True))
    across = lax.rsqrt(jnp.sum(on_diag, 0, keepdims=True))
    scaled = gram * down * across
    bound = jnp.minimum(
        jnp.max(jnp.sum(jnp.abs(scaled), 0, keepdims=True)),
        jnp.sqrt(jnp.sum(scaled * scaled)),
    )
    step = 1.9 / bound
    error = eye - step * scaled
    inverse = step * eye

    def more(state):
        count, size, _, _ = state
        return jnp.logical_and(count < 40, size > 1e-4)

    def double(state):
        count, _, inverse, error = state
        size = jnp.sum(error * error)
        return count + 1, size, inverse + dot3(inverse, error), dot3(error, error)

    _, _, inverse, _ = lax.while_loop(more, double, (0, jnp.float32(1.0), inverse, error))

    def again(state):
        count, size, _ = state
        return jnp.logical_and(count < 20, size > 1e-6)

    def refine(state):
        count, _, inverse = state
        rest = eye - dot6(scaled, inverse)
        return count + 1, jnp.sum(rest * rest), inverse + dot3(inverse, rest)

    _, _, inverse = lax.while_loop(again, refine, (0, jnp.float32(1.0), inverse))
    out_ref[...] = down * dot6(inverse, down * right_ref[...])


def solve(gram, right):
    return pl.pallas_call(
        solve_kernel,
        out_shape=jax.ShapeDtypeStruct(right.shape, jnp.float32),
        compiler_params=pltpu.CompilerParams(vmem_limit_bytes=32 << 20),
    )(gram, right)


def per_device(n_tm, n_rows, snapshots, right_basis, threshold):
    rows, rank = snapshots.shape[0], right_basis.shape[1]
    me = lax.axis_index("tm")
    blocks = n_tm // 2
    low = 0
    for b in range(blocks.bit_length() - 1):
        low = low * 2 + (me >> b) % 2
    data = reorder(snapshots, low, blocks)
    residual = data
    part = rows // CHUNKS
    weights = right_basis.T
    for iteration in range(ITERS):
        chunks = [mm(residual[i * part : (i + 1) * part], weights, NT) for i in range(CHUNKS)]
        chunks = sum_tm(chunks, n_tm)
        products = 0.0
        for i, left in enumerate(chunks):
            products += jnp.concatenate(
                [mm(left, left, TN, highest), mm(left, residual[i * part : (i + 1) * part], TN)], 1
            )
        products = sum_rows(products, n_rows)
        weights = solve(products[:, :rank], products[:, rank:])
        low_rank = jnp.concatenate([mm(left, weights, NN) for left in chunks], 0)
        difference = data - low_rank
        sparse = jnp.sign(difference) * jnp.maximum(jnp.abs(difference) - threshold[None, :], 0.0)
        residual = data - sparse
    return reorder(low_rank, low, blocks), reorder(sparse, low, blocks)


def solution(mesh):
    return jax.shard_map(
        functools.partial(per_device, mesh.shape["tm"], mesh.shape["rows"]),
        mesh=mesh,
        in_specs=(P("rows", "tm"), P("tm", None), P("tm")),
        out_specs=(P("rows", "tm"), P("rows", "tm")),
        check_vma=False,
    )
```

```python
import functools
import jax
import jax.numpy as jnp
from jax import lax
from jax.experimental import pallas as pl
from jax.experimental.pallas import tpu as pltpu
from jax.sharding import PartitionSpec as P

ITERS = 2
CHUNKS = 4
VMEM_BYTES = 28 << 20

NN = (((1,), (0,)), ((), ()))
NT = (((1,), (1,)), ((), ()))
TN = (((0,), (0,)), ((), ()))
f32, bf16 = jnp.float32, jnp.bfloat16


def split(x, terms):
    out = []
    for _ in range(terms):
        out.append(x.astype(bf16))
        x = x - out[-1].astype(f32)
    return out


def dot(a, b, dims=NN):
    return lax.dot_general(a, b, dims, preferred_element_type=f32)


def dot3(a, b, dims=NN):
    return dot(a[0], b[0], dims) + (dot(a[0], b[1], dims) + dot(a[1], b[0], dims))


def dot6(a, b):
    small = dot(a[0], b[2]) + dot(a[1], b[1]) + dot(a[2], b[0])
    return dot(a[0], b[0]) + (dot(a[0], b[1]) + dot(a[1], b[0]) + small)


def swap(x, axis, size, bit):
    return lax.ppermute(x, axis, [(i, i ^ bit) for i in range(size)])


def bits_of(size):
    return [1 << b for b in range(size.bit_length() - 1)]


def sum_tm(chunks, size):
    first, *middle, last = bits_of(size)
    chunks = [kept + swap(sent, "tm", size, first) for kept, sent in chunks]
    for bit in middle:
        for i, x in enumerate(chunks):
            half = x.shape[0] // 2
            chunks[i] = x[:half] + swap(x[half:], "tm", size, bit)
    pieces = []
    for x in chunks:
        x = x + swap(x, "tm", size, last)
        parts = [x]
        for bit in reversed(middle):
            x = parts[0] if len(parts) == 1 else jnp.concatenate(parts, 0)
            parts.append(swap(x, "tm", size, bit))
        pieces.append(parts + [swap(x, "tm", size, first) for x in parts])
    return pieces


def sum_rows(a, b, size):
    bits = bits_of(size)
    turn = len(bits) // 2
    pair_a, pair_b = None, None
    for bit_a, bit_b in zip(bits, bits[turn:] + bits[:turn]):
        a = a if pair_a is None else pair_a[0] + pair_a[1]
        b = b if pair_b is None else pair_b[0] + pair_b[1]
        pair_a, pair_b = (a, swap(a, "rows", size, bit_a)), (b, swap(b, "rows", size, bit_b))
    return pair_a + pair_b


def lowest(blocks):
    me = lax.axis_index("tm")
    low = 0
    for b in range(blocks.bit_length() - 1):
        low = low * 2 + lax.rem(me >> b, 2)
    return low


def write_left(left, out_refs, blocks):
    tall = left[0].shape[0]
    share = tall // CHUNKS
    for p in range(blocks):
        for c in range(CHUNKS):
            at = p % (blocks // 2) * share
            out_refs[2 * c + p // (blocks // 2)][pl.ds(at, share), :] = left[p][c * share : (c + 1) * share]


def head_kernel(blocks, snap_ref, basis_ref, data_ref, top_ref, rest_ref, *more):
    *left_refs, sems = more
    tall = data_ref.shape[0] // blocks
    low = lowest(blocks)
    copies = []
    for p in range(blocks):
        copies.append(
            pltpu.make_async_copy(
                snap_ref.at[pl.ds(pl.multiple_of((p ^ low) * tall, tall), tall), :],
                data_ref.at[pl.ds(p * tall, tall), :],
                sems.at[p],
            )
        )
        copies[-1].start()
    basis = split(basis_ref[...], 2)
    left = []
    for p in range(blocks):
        copies[p].wait()
        block = split(data_ref[pl.ds(p * tall, tall), :], 2)
        top_ref[pl.ds(p * tall, tall), :], rest_ref[pl.ds(p * tall, tall), :] = block
        left.append(dot3(block, basis))
    write_left(left, left_refs, blocks)


def product_kernel(blocks, counts, top_ref, rest_ref, *more):
    left_refs, (a_ref, b_ref, left_top_ref, left_rest_ref) = more[:-4], more[-4:]
    rows, rank = left_top_ref.shape
    tall = rows // blocks
    share = tall // CHUNKS
    at = 0
    for c in range(CHUNKS):
        p = 0
        for ref in left_refs[at : at + counts[c]]:
            terms = split(ref[...], 2)
            for k in range(ref.shape[0] // share):
                for out_ref, term in zip((left_top_ref, left_rest_ref), terms):
                    out_ref[pl.ds(p * tall + c * share, share), :] = term[k * share : (k + 1) * share]
                p += 1
        at += counts[c]
    left = left_top_ref[...], left_rest_ref[...]
    right = dot3(left, (top_ref[...], rest_ref[...]), TN)
    cross = dot(left[0], left[1], TN)
    gram = dot(left[0], left[0], TN) + (cross + cross.T)
    half = rank // 2
    a_ref[:, : right.shape[1]] = right[:half]
    b_ref[:, : right.shape[1]] = right[half:]
    a_ref[:, right.shape[1] :] = gram[:half]
    b_ref[:, right.shape[1] :] = gram[half:]


def solve(gram, right):
    n = gram.shape[0]
    eye = (
        lax.broadcasted_iota(jnp.int32, (n, n), 0) == lax.broadcasted_iota(jnp.int32, (n, n), 1)
    ).astype(f32)
    on_diag = gram * eye
    down = lax.rsqrt(jnp.sum(on_diag, 1, keepdims=True))
    across = lax.rsqrt(jnp.sum(on_diag, 0, keepdims=True))
    scaled = gram * down * across
    bound = jnp.minimum(
        jnp.max(jnp.sum(jnp.abs(scaled), 0, keepdims=True)),
        jnp.sqrt(jnp.sum(scaled * scaled)),
    )
    step = 1.9 / bound
    error = eye - step * scaled
    inverse = step * eye

    def more(state):
        count, size, _, _ = state
        return jnp.logical_and(count < 40, size > 1e-4)

    def double(state):
        count, _, inverse, error = state
        size = jnp.sum(error * error)
        terms = split(error, 2)
        return count + 1, size, inverse + dot3(split(inverse, 2), terms), dot3(terms, terms)

    _, _, inverse, _ = lax.while_loop(more, double, (0, jnp.float32(1.0), inverse, error))
    exact = split(scaled, 3)

    def again(state):
        count, size, _ = state
        return jnp.logical_and(count < 20, size > 1e-6)

    def refine(state):
        count, _, inverse = state
        rest = eye - dot6(exact, split(inverse, 3))
        return count + 1, jnp.sum(rest * rest), inverse + dot3(split(inverse, 2), split(rest, 2))

    _, _, inverse = lax.while_loop(again, refine, (0, jnp.float32(1.0), inverse))
    return down * dot6(split(inverse, 3), split(down * right, 3))


def weights_of(sum_refs, cols):
    a = sum_refs[0][...] + sum_refs[1][...]
    b = sum_refs[2][...] + sum_refs[3][...]
    both = jnp.concatenate([a, b], 0)
    return solve(both[:, cols:], both[:, :cols])


def shrink(data, low_rank, level):
    difference = data - low_rank
    size = jnp.maximum(jnp.abs(difference) - level, 0.0)
    return jnp.where(difference < 0, -size, size)


def middle_kernel(blocks, *refs):
    sum_refs, refs = refs[:4], refs[4:]
    left_top_ref, left_rest_ref, data_ref, level_ref, top_ref, rest_ref, *left_refs = refs
    tall = data_ref.shape[0] // blocks
    weights = split(weights_of(sum_refs, data_ref.shape[1]), 2)
    left = []
    for p in range(blocks):
        at = pl.ds(p * tall, tall)
        low_rank = dot3((left_top_ref[at, :], left_rest_ref[at, :]), weights)
        data = data_ref[at, :]
        residual = split(data - shrink(data, low_rank, level_ref[...]), 2)
        top_ref[at, :], rest_ref[at, :] = residual
        left.append(dot3(residual, weights, NT))
    write_left(left, left_refs, blocks)


def last_kernel(blocks, *refs):
    sum_refs, refs = refs[:4], refs[4:]
    left_top_ref, left_rest_ref, data_ref, level_ref, low_rank_ref, sparse_ref, low_rank, sparse, sems = refs
    tall = data_ref.shape[0] // blocks
    low = lowest(blocks)
    weights = split(weights_of(sum_refs, data_ref.shape[1]), 2)
    copies = []
    for p in range(blocks):
        at = pl.ds(p * tall, tall)
        low_rank[at, :] = dot3((left_top_ref[at, :], left_rest_ref[at, :]), weights)
        sparse[at, :] = shrink(data_ref[at, :], low_rank[at, :], level_ref[...])
        to = pl.ds(pl.multiple_of((p ^ low) * tall, tall), tall)
        for k, (source, target) in enumerate(((low_rank, low_rank_ref), (sparse, sparse_ref))):
            copies.append(pltpu.make_async_copy(source.at[at, :], target.at[to, :], sems.at[2 * p + k]))
            copies[-1].start()
    for copy in copies:
        copy.wait()


VMEM = pl.BlockSpec(memory_space=pltpu.VMEM)
ANY = pl.BlockSpec(memory_space=pl.ANY)


def call(body, args, outs, in_specs=None, out_specs=None, scratch=(), name=None):
    return pl.pallas_call(
        body,
        out_shape=[jax.ShapeDtypeStruct(shape, dtype) for shape, dtype in outs],
        in_specs=in_specs or [VMEM] * len(args),
        out_specs=out_specs or [VMEM] * len(outs),
        scratch_shapes=list(scratch),
        compiler_params=pltpu.CompilerParams(vmem_limit_bytes=VMEM_BYTES),
        name=name,
    )(*args)


def per_device(n_tm, n_rows, snapshots, right_basis, threshold):
    rows, cols = snapshots.shape
    rank = right_basis.shape[1]
    blocks = n_tm // 2
    level = threshold[None, :]
    whole = [((rows, cols), bf16)] * 2
    lefts = [((rows // CHUNKS // 2, rank), f32)] * (2 * CHUNKS)
    data, top, rest, *left = call(
        functools.partial(head_kernel, blocks),
        (snapshots, right_basis),
        [((rows, cols), f32)] + whole + lefts,
        in_specs=[ANY, VMEM],
        scratch=[pltpu.SemaphoreType.DMA((blocks,))],
        name="head",
    )
    for iteration in range(ITERS):
        pieces = sum_tm(list(zip(left[::2], left[1::2])), n_tm)
        a, b, left_top, left_rest = call(
            functools.partial(product_kernel, blocks, [len(x) for x in pieces]),
            (top, rest, *[x for parts in pieces for x in parts]),
            [((rank // 2, cols + rank), f32)] * 2 + [((rows, rank), bf16)] * 2,
            name="products",
        )
        args = (*sum_rows(a, b, n_rows), left_top, left_rest, data, level)
        if iteration < ITERS - 1:
            top, rest, *left = call(
                functools.partial(middle_kernel, blocks), args, whole + lefts, name="middle"
            )
    return call(
        functools.partial(last_kernel, blocks),
        args,
        [((rows, cols), f32)] * 2,
        out_specs=[ANY] * 2,
        scratch=[pltpu.VMEM((rows, cols), f32)] * 2 + [pltpu.SemaphoreType.DMA((2 * blocks,))],
        name="last",
    )


def solution(mesh):
    return jax.shard_map(
        functools.partial(per_device, mesh.shape["tm"], mesh.shape["rows"]),
        mesh=mesh,
        in_specs=(P("rows", "tm"), P("tm", None), P("tm")),
        out_specs=(P("rows", "tm"), P("rows", "tm")),
        check_vma=False,
    )
```

```python
import functools
import jax
import jax.numpy as jnp
from jax import lax
from jax.experimental import pallas as pl
from jax.experimental.pallas import tpu as pltpu
from jax.sharding import PartitionSpec as P

ITERS = 2
CHUNKS = 4
SUBLANES = 8
VMEM_BYTES = 16 << 20

NN = (((1,), (0,)), ((), ()))
NT = (((1,), (1,)), ((), ()))
TN = (((0,), (0,)), ((), ()))
f32, bf16 = jnp.float32, jnp.bfloat16


def split(x, terms):
    out = []
    for _ in range(terms):
        out.append(x.astype(bf16))
        x = x - out[-1].astype(f32)
    return out


def dot(a, b, dims=NN):
    return lax.dot_general(a, b, dims, preferred_element_type=f32)


def dot3(a, b, dims=NN):
    return dot(a[0], b[0], dims) + (dot(a[0], b[1], dims) + dot(a[1], b[0], dims))


def dot6(a, b):
    small = dot(a[0], b[2]) + dot(a[1], b[1]) + dot(a[2], b[0])
    return dot(a[0], b[0]) + (dot(a[0], b[1]) + dot(a[1], b[0]) + small)


def swap(x, axis, size, bit):
    return lax.ppermute(x, axis, [(i, i ^ bit) for i in range(size)])


def bits_of(size):
    return [1 << b for b in range(size.bit_length() - 1)]


def sum_tm(chunks, size):
    first, *middle, last = bits_of(size)
    chunks = [kept + swap(sent, "tm", size, first) for kept, sent in chunks]
    for bit in middle:
        for i, x in enumerate(chunks):
            half = x.shape[0] // 2
            chunks[i] = x[:half] + swap(x[half:], "tm", size, bit)
    pieces = []
    for x in chunks:
        x = x + swap(x, "tm", size, last)
        parts = [x]
        for bit in reversed(middle):
            x = parts[0] if len(parts) == 1 else jnp.concatenate(parts, 0)
            parts.append(swap(x, "tm", size, bit))
        pieces.append(parts + [swap(x, "tm", size, first) for x in parts])
    return pieces


def sum_rows(a, b, size):
    bits = bits_of(size)
    turn = len(bits) // 2
    pair_a, pair_b = None, None
    for bit_a, bit_b in zip(bits, bits[turn:] + bits[:turn]):
        a = a if pair_a is None else pair_a[0] + pair_a[1]
        b = b if pair_b is None else pair_b[0] + pair_b[1]
        pair_a, pair_b = (a, swap(a, "rows", size, bit_a)), (b, swap(b, "rows", size, bit_b))
    return pair_a + pair_b


def lowest(blocks):
    me = lax.axis_index("tm")
    low = 0
    for b in range(blocks.bit_length() - 1):
        low = low * 2 + lax.rem(me >> b, 2)
    return low


def write_left(left, out_refs, blocks):
    tall = left[0].shape[0]
    share = tall // CHUNKS
    for p in range(blocks):
        for c in range(CHUNKS):
            at = p % (blocks // 2) * share
            out_refs[2 * c + p // (blocks // 2)][pl.ds(at, share), :] = left[p][c * share : (c + 1) * share]


def head_kernel(blocks, snap_ref, basis_ref, data_ref, top_ref, rest_ref, *more):
    *left_refs, sems = more
    tall = data_ref.shape[0] // blocks
    low = lowest(blocks)
    copies = []
    for p in range(blocks):
        copies.append(
            pltpu.make_async_copy(
                snap_ref.at[pl.ds(pl.multiple_of((p ^ low) * tall, tall), tall), :],
                data_ref.at[pl.ds(p * tall, tall), :],
                sems.at[p],
            )
        )
        copies[-1].start()
    basis = split(basis_ref[...], 2)
    left = []
    for p in range(blocks):
        copies[p].wait()
        block = split(data_ref[pl.ds(p * tall, tall), :], 2)
        top_ref[pl.ds(p * tall, tall), :], rest_ref[pl.ds(p * tall, tall), :] = block
        left.append(dot3(block, basis))
    write_left(left, left_refs, blocks)


def product_kernel(blocks, counts, top_ref, rest_ref, *more):
    left_refs, (a_ref, b_ref, left_top_ref, left_rest_ref) = more[:-4], more[-4:]
    rows, rank = left_top_ref.shape
    tall = rows // blocks
    share = tall // CHUNKS
    at = 0
    for c in range(CHUNKS):
        p = 0
        for ref in left_refs[at : at + counts[c]]:
            terms = split(ref[...], 2)
            for k in range(ref.shape[0] // share):
                for out_ref, term in zip((left_top_ref, left_rest_ref), terms):
                    out_ref[pl.ds(p * tall + c * share, share), :] = term[k * share : (k + 1) * share]
                p += 1
        at += counts[c]
    left = left_top_ref[...], left_rest_ref[...]
    right = dot3(left, (top_ref[...], rest_ref[...]), TN)
    cross = dot(left[0], left[1], TN)
    gram = dot(left[0], left[0], TN) + (cross + cross.T)
    pack(gram, right, a_ref, b_ref)


def pack(gram, right, a_ref, b_ref):
    half = gram.shape[0] // 2
    lower = below(half)
    a_ref[:half, :half] = jnp.where(lower, gram[:half, :half], gram[half:, half:])
    a_ref[:half, half:] = gram[half:, :half]
    diagonal = jnp.sum(jnp.where(identity(half), gram[half:, half:], 0.0), 0, keepdims=True)
    a_ref[half : half + SUBLANES, :] = jnp.broadcast_to(
        jnp.concatenate([diagonal, diagonal], 1), (SUBLANES, 2 * half)
    )
    taken = a_ref.shape[0] - half - SUBLANES
    a_ref[half + SUBLANES :, :] = right[:taken]
    b_ref[...] = right[taken:]


def unpack_gram(a):
    half = a.shape[1] // 2
    lower = below(half)
    both, off = a[:half, :half], a[:half, half:]
    turned = both.T
    first = jnp.where(lower, both, turned)
    second = jnp.where(identity(half), a[half : half + 1, :half], jnp.where(lower, turned, both))
    return jnp.concatenate([jnp.concatenate([first, off.T], 1), jnp.concatenate([off, second], 1)], 0)


def unpack_right(a, b):
    return jnp.concatenate([a[a.shape[1] // 2 + SUBLANES :], b], 0)


def identity(n):
    return lax.broadcasted_iota(jnp.int32, (n, n), 0) == lax.broadcasted_iota(jnp.int32, (n, n), 1)


def below(n):
    return lax.broadcasted_iota(jnp.int32, (n, n), 0) >= lax.broadcasted_iota(jnp.int32, (n, n), 1)


def norm_bound(x):
    size = jnp.abs(x)
    return jnp.minimum(jnp.max(jnp.sum(size, 0, keepdims=True)), jnp.max(jnp.sum(size, 1, keepdims=True)))


def converge(inverse, error, enough):
    def more(state):
        count, size, _, _ = state
        return jnp.logical_and(count < 40, size > enough)

    def double(state):
        count, _, inverse, error = state
        size = jnp.sum(error * error)
        terms = split(error, 2)
        return count + 1, size, inverse + dot3(split(inverse, 2), terms), dot3(terms, terms)

    _, size, inverse, _ = lax.while_loop(more, double, (0, jnp.float32(1e9), inverse, error))
    return inverse, size


def diagonals(gram):
    on_diag = jnp.where(identity(gram.shape[0]), gram, 0.0)
    return jnp.sum(on_diag, 1, keepdims=True), jnp.sum(on_diag, 0, keepdims=True)


def plain_start(scaled):
    eye = identity(scaled.shape[0]).astype(f32)
    step = 1.9 / norm_bound(scaled)
    return step * eye, eye - step * scaled


def inverse_kernel(a_ref, out_ref, size_ref):
    gram = unpack_gram(a_ref[...])
    down, across = diagonals(gram)
    down, across = lax.rsqrt(down), lax.rsqrt(across)
    inverse, size = converge(*plain_start(gram * down * across), 1e-2)
    out_ref[...] = inverse * down * across
    size_ref[...] = jnp.full(size_ref.shape, size)


def solve(gram, right, start, start_size):
    down, across = diagonals(gram)
    start = start * jnp.sqrt(down) * jnp.sqrt(across)
    down, across = lax.rsqrt(down), lax.rsqrt(across)
    scaled = gram * down * across
    right = right * down
    exact = split(scaled, 3)
    eye = identity(gram.shape[0]).astype(f32)
    product = dot6(exact, split(start, 3))
    terms = split(product, 2)
    square = dot3(terms, terms)
    bound = jnp.minimum(norm_bound(product), jnp.sqrt(norm_bound(square)))
    good = jnp.logical_and(start_size <= 1e-2, bound < 1e3)
    step = 2.0 / (1.0 + bound)

    def from_start():
        error = eye - (2.0 * step) * product + (step * step) * square
        return (2.0 * step) * start - (step * step) * dot3(split(start, 2), terms), error

    inverse, error = lax.cond(good, from_start, lambda: plain_start(scaled))
    inverse, _ = converge(inverse, error, 1e-4)
    factors = split(inverse, 2)
    out = dot3(factors, split(right, 2))
    scale = jnp.sum(right * right)

    def again(state):
        count, size, _ = state
        return jnp.logical_and(count < 20, size > 1e-6 * scale)

    def refine(state):
        count, _, out = state
        rest = right - dot6(exact, split(out, 3))
        return count + 1, jnp.sum(rest * rest), out + dot3(factors, split(rest, 2))

    _, _, out = lax.while_loop(again, refine, (0, 2.0 * scale, out))
    return out * down


def weights_of(refs):
    a1_ref, a2_ref, b1_ref, b2_ref, start_ref, size_ref = refs
    a, b = a1_ref[...] + a2_ref[...], b1_ref[...] + b2_ref[...]
    return solve(unpack_gram(a), unpack_right(a, b), start_ref[...], jnp.max(size_ref[...]))


def shrink(data, low_rank, level):
    difference = data - low_rank
    size = jnp.maximum(jnp.abs(difference) - level, 0.0)
    return jnp.where(difference < 0, -size, size)


def middle_kernel(blocks, *refs):
    sum_refs, refs = refs[:6], refs[6:]
    left_top_ref, left_rest_ref, data_ref, level_ref, top_ref, rest_ref, *left_refs = refs
    tall = data_ref.shape[0] // blocks
    weights = split(weights_of(sum_refs), 2)
    left = []
    for p in range(blocks):
        at = pl.ds(p * tall, tall)
        low_rank = dot3((left_top_ref[at, :], left_rest_ref[at, :]), weights)
        data = data_ref[at, :]
        residual = split(data - shrink(data, low_rank, level_ref[...]), 2)
        top_ref[at, :], rest_ref[at, :] = residual
        left.append(dot3(residual, weights, NT))
    write_left(left, left_refs, blocks)


def last_kernel(blocks, *refs):
    sum_refs, refs = refs[:6], refs[6:]
    left_top_ref, left_rest_ref, data_ref, level_ref, low_rank_ref, sparse_ref, low_rank, sparse, sems = refs
    tall = data_ref.shape[0] // blocks
    low = lowest(blocks)
    weights = split(weights_of(sum_refs), 2)
    copies = []
    for p in range(blocks):
        at = pl.ds(p * tall, tall)
        low_rank[at, :] = dot3((left_top_ref[at, :], left_rest_ref[at, :]), weights)
        sparse[at, :] = shrink(data_ref[at, :], low_rank[at, :], level_ref[...])
        to = pl.ds(pl.multiple_of((p ^ low) * tall, tall), tall)
        for k, (source, target) in enumerate(((low_rank, low_rank_ref), (sparse, sparse_ref))):
            copies.append(pltpu.make_async_copy(source.at[at, :], target.at[to, :], sems.at[2 * p + k]))
            copies[-1].start()
    for copy in copies:
        copy.wait()


VMEM = pl.BlockSpec(memory_space=pltpu.VMEM)
ANY = pl.BlockSpec(memory_space=pl.ANY)


def call(body, args, outs, in_specs=None, out_specs=None, scratch=(), cost=None, name=None):
    return pl.pallas_call(
        body,
        out_shape=[jax.ShapeDtypeStruct(shape, dtype) for shape, dtype in outs],
        in_specs=in_specs or [VMEM] * len(args),
        out_specs=out_specs or [VMEM] * len(outs),
        scratch_shapes=list(scratch),
        compiler_params=pltpu.CompilerParams(vmem_limit_bytes=VMEM_BYTES),
        cost_estimate=cost,
        name=name,
    )(*args)


def per_device(n_tm, n_rows, snapshots, right_basis, threshold):
    rows, cols = snapshots.shape
    rank = right_basis.shape[1]
    blocks = n_tm // 2
    level = threshold[None, :]
    whole = [((rows, cols), bf16)] * 2
    a_rows = (rank + rank // 2 + SUBLANES) // 16 * 8 + SUBLANES
    lefts = [((rows // CHUNKS // 2, rank), f32)] * (2 * CHUNKS)
    data, top, rest, *left = call(
        functools.partial(head_kernel, blocks),
        (snapshots, right_basis),
        [((rows, cols), f32)] + whole + lefts,
        in_specs=[ANY, VMEM],
        scratch=[pltpu.SemaphoreType.DMA((blocks,))],
        name="head",
    )
    for iteration in range(ITERS):
        pieces = sum_tm(list(zip(left[::2], left[1::2])), n_tm)
        a, b, left_top, left_rest = call(
            functools.partial(product_kernel, blocks, [len(x) for x in pieces]),
            (top, rest, *[x for parts in pieces for x in parts]),
            [((a_rows, cols), f32), ((rank + rank // 2 + SUBLANES - a_rows, cols), f32)] + [((rows, rank), bf16)] * 2,
            name="products",
        )
        sums = sum_rows(a, b, n_rows)
        start = call(
            inverse_kernel,
            sums[:1],
            [((rank, rank), f32), ((SUBLANES, 128), f32)],
            cost=pl.CostEstimate(flops=80 * rank**3, bytes_accessed=rank * rank * 8, transcendentals=0),
            name="inverse",
        )
        args = (*sums, *start, left_top, left_rest, data, level)
        if iteration < ITERS - 1:
            top, rest, *left = call(
                functools.partial(middle_kernel, blocks), args, whole + lefts, name="middle"
            )
    return call(
        functools.partial(last_kernel, blocks),
        args,
        [((rows, cols), f32)] * 2,
        out_specs=[ANY] * 2,
        scratch=[pltpu.VMEM((rows, cols), f32)] * 2 + [pltpu.SemaphoreType.DMA((2 * blocks,))],
        name="last",
    )


def solution(mesh):
    return jax.shard_map(
        functools.partial(per_device, mesh.shape["tm"], mesh.shape["rows"]),
        mesh=mesh,
        in_specs=(P("rows", "tm"), P("tm", None), P("tm")),
        out_specs=(P("rows", "tm"), P("rows", "tm")),
        check_vma=False,
    )
```

```python
import functools
import jax
import jax.numpy as jnp
from jax import lax
from jax.experimental import pallas as pl
from jax.experimental.pallas import tpu as pltpu
from jax.sharding import PartitionSpec as P

ITERS = 2
CHUNKS = 4
SUBLANES = 8
LOW = 1e-3
NEAR, FAR = 1.25, 4.2
VMEM_BYTES = 16 << 20

NN = (((1,), (0,)), ((), ()))
NT = (((1,), (1,)), ((), ()))
TN = (((0,), (0,)), ((), ()))
f32, bf16 = jnp.float32, jnp.bfloat16


def split(x, terms):
    out = []
    for _ in range(terms):
        out.append(x.astype(bf16))
        x = x - out[-1].astype(f32)
    return out


def dot(a, b, dims=NN):
    return lax.dot_general(a, b, dims, preferred_element_type=f32)


def dot3(a, b, dims=NN):
    return dot(a[0], b[0], dims) + (dot(a[0], b[1], dims) + dot(a[1], b[0], dims))


def dot6(a, b):
    small = dot(a[0], b[2]) + dot(a[1], b[1]) + dot(a[2], b[0])
    return dot(a[0], b[0]) + (dot(a[0], b[1]) + dot(a[1], b[0]) + small)


def swap(x, axis, size, bit):
    return lax.ppermute(x, axis, [(i, i ^ bit) for i in range(size)])


def bits_of(size):
    return [1 << b for b in range(size.bit_length() - 1)]


def sum_tm(chunks, size):
    first, *middle, last = bits_of(size)
    chunks = [kept + swap(sent, "tm", size, first) for kept, sent in chunks]
    for bit in middle:
        for i, x in enumerate(chunks):
            half = x.shape[0] // 2
            chunks[i] = x[:half] + swap(x[half:], "tm", size, bit)
    pieces = []
    for x in chunks:
        x = x + swap(x, "tm", size, last)
        parts = [x]
        for bit in reversed(middle):
            x = parts[0] if len(parts) == 1 else jnp.concatenate(parts, 0)
            parts.append(swap(x, "tm", size, bit))
        pieces.append(parts + [swap(x, "tm", size, first) for x in parts])
    return pieces


def sum_rows(a, b, size):
    bits = bits_of(size)
    turn = len(bits) // 2
    pair_a, pair_b = None, None
    for bit_a, bit_b in zip(bits, bits[turn:] + bits[:turn]):
        a = a if pair_a is None else pair_a[0] + pair_a[1]
        b = b if pair_b is None else pair_b[0] + pair_b[1]
        pair_a, pair_b = (a, swap(a, "rows", size, bit_a)), (b, swap(b, "rows", size, bit_b))
    return pair_a + pair_b


def lowest(blocks):
    me = lax.axis_index("tm")
    low = 0
    for b in range(blocks.bit_length() - 1):
        low = low * 2 + lax.rem(me >> b, 2)
    return low


def write_left(left, out_refs, blocks):
    tall = left[0].shape[0]
    share = tall // CHUNKS
    for p in range(blocks):
        for c in range(CHUNKS):
            at = p % (blocks // 2) * share
            out_refs[2 * c + p // (blocks // 2)][pl.ds(at, share), :] = left[p][c * share : (c + 1) * share]


def fetches(snap_ref, data, sems, blocks):
    tall = data.shape[0] // blocks
    low = lowest(blocks)
    return [
        pltpu.make_async_copy(
            snap_ref.at[pl.ds(pl.multiple_of((p ^ low) * tall, tall), tall), :],
            data.at[pl.ds(p * tall, tall), :],
            sems.at[p],
        )
        for p in range(blocks)
    ]


def head_kernel(blocks, snap_ref, basis_ref, data, top_ref, rest_ref, *more):
    *left_refs, basis, sems, basis_sem = more
    tall = data.shape[0] // blocks
    copies = fetches(snap_ref, data, sems, blocks)
    first = pltpu.make_async_copy(basis_ref, basis, basis_sem)
    first.start()
    for copy in copies:
        copy.start()
    first.wait()
    basis = split(basis[...], 2)
    left = []
    for p in range(blocks):
        at = pl.ds(p * tall, tall)
        copies[p].wait()
        top_ref[at, :], rest_ref[at, :] = block = split(data[at, :], 2)
        left.append(dot3(block, basis))
    write_left(left, left_refs, blocks)


def product_kernel(blocks, counts, top_ref, rest_ref, *more):
    left_refs, (a_ref, b_ref, left_top_ref, left_rest_ref) = more[:-4], more[-4:]
    rows, rank = left_top_ref.shape
    tall = rows // blocks
    share = tall // CHUNKS
    at = 0
    for c in range(CHUNKS):
        p = 0
        for ref in left_refs[at : at + counts[c]]:
            terms = split(ref[...], 2)
            for k in range(ref.shape[0] // share):
                for out_ref, term in zip((left_top_ref, left_rest_ref), terms):
                    out_ref[pl.ds(p * tall + c * share, share), :] = term[k * share : (k + 1) * share]
                p += 1
        at += counts[c]
    left = left_top_ref[...], left_rest_ref[...]
    right = dot3(left, (top_ref[...], rest_ref[...]), TN)
    cross = dot(left[0], left[1], TN)
    gram = dot(left[0], left[0], TN) + (cross + cross.T + dot(left[1], left[1], TN))
    pack(gram, right, a_ref, b_ref)


def pack(gram, right, a_ref, b_ref):
    half = gram.shape[0] // 2
    lower = below(half)
    a_ref[:half, :half] = jnp.where(lower, gram[:half, :half], gram[half:, half:])
    a_ref[:half, half:] = gram[half:, :half]
    diagonal = jnp.sum(jnp.where(identity(half), gram[half:, half:], 0.0), 0, keepdims=True)
    a_ref[half : half + SUBLANES, :] = jnp.broadcast_to(
        jnp.concatenate([diagonal, diagonal], 1), (SUBLANES, 2 * half)
    )
    taken = a_ref.shape[0] - half - SUBLANES
    a_ref[half + SUBLANES :, :] = right[:taken]
    b_ref[...] = right[taken:]


def unpack_gram(a):
    half = a.shape[1] // 2
    lower = below(half)
    both, off = a[:half, :half], a[:half, half:]
    turned = both.T
    first = jnp.where(lower, both, turned)
    second = jnp.where(identity(half), a[half : half + 1, :half], jnp.where(lower, turned, both))
    return jnp.concatenate([jnp.concatenate([first, off.T], 1), jnp.concatenate([off, second], 1)], 0)


def unpack_right(a, b):
    return jnp.concatenate([a[a.shape[1] // 2 + SUBLANES :], b], 0)


def identity(n):
    return lax.broadcasted_iota(jnp.int32, (n, n), 0) == lax.broadcasted_iota(jnp.int32, (n, n), 1)


def below(n):
    return lax.broadcasted_iota(jnp.int32, (n, n), 0) >= lax.broadcasted_iota(jnp.int32, (n, n), 1)


def norm_bound(x):
    return jnp.max(jnp.sum(jnp.abs(x), 0, keepdims=True))


def chebyshev(matrix, square, low, high):
    at_zero, slope = (high + low) / (high - low), 2.0 / (high - low)
    growth = 2.0 * at_zero * at_zero - 1.0
    a, b = 4.0 * at_zero * slope / growth, 2.0 * slope * slope / growth
    return a, b, identity(matrix.shape[0]).astype(f32) - a * matrix + b * square, growth


def double(inverse, error, growth):
    growth = 2.0 * growth * growth - 1.0
    eye = identity(error.shape[0]).astype(f32)
    terms = split(error, 2)
    inverse = (1.0 + 1.0 / growth) * (inverse + dot3(split(inverse, 2), terms))
    error = (1.0 + 1.0 / growth) * dot3(terms, terms) - (1.0 / growth) * eye
    return inverse, error, growth


def converge(inverse, error, growth, enough):
    def more(state):
        count, size, *_ = state
        return jnp.logical_and(count < 40, size > enough)

    def body(state):
        count, _, *state = state
        inverse, error, growth = double(*state)
        return count + 1, jnp.sum(state[1] * state[1]), inverse, error, jnp.minimum(growth, 1e4)

    _, size, inverse, *_ = lax.while_loop(more, body, (0, jnp.float32(1e9), inverse, error, growth))
    return inverse, size


def diagonals(gram):
    on_diag = jnp.where(identity(gram.shape[0]), gram, 0.0)
    return jnp.sum(on_diag, 1, keepdims=True), jnp.sum(on_diag, 0, keepdims=True)


def invert(scaled, enough):
    terms = split(scaled, 2)
    eye = identity(scaled.shape[0]).astype(f32)
    high = norm_bound(scaled)
    a, b, error, growth = chebyshev(scaled, dot3(terms, terms), LOW * high, high)
    return converge(a * eye - b * scaled, error, growth, enough)


def inverse_kernel(a_ref, level_ref, out_ref, level_out_ref):
    level_out_ref[...] = level_ref[...]
    gram = unpack_gram(a_ref[...])
    down, across = diagonals(gram)
    down, across = lax.rsqrt(down), lax.rsqrt(across)
    out_ref[...] = invert(gram * down * across, 0.5)[0] * down * across


def refine(exact, factors, right, scale, out):
    def again(state):
        count, size, _ = state
        return jnp.logical_and(count < 60, size > 2e-5 * scale)

    def body(state):
        count, _, out = state
        rest = right - dot6(exact, split(out, 3))
        return count + 1, jnp.sum(rest * rest), out + dot3(factors, split(rest, 2))

    return lax.while_loop(again, body, (0, 2.0 * scale, out))[1:]


def solve(gram, right, start):
    down, across = diagonals(gram)
    start = start * jnp.sqrt(down) * jnp.sqrt(across)
    down, across = lax.rsqrt(down), lax.rsqrt(across)
    scaled = gram * down * across
    right = right * down
    scale = jnp.sum(right * right)
    exact = split(scaled, 3)
    product = dot6(exact, split(start, 3))
    terms = split(product, 2)
    follow = dot3(split(start, 2), terms)
    a, b, error, growth = chebyshev(product, dot3(terms, terms), NEAR, FAR)
    inverse = a * start - b * follow
    while growth < 1e3:
        inverse, error, growth = double(inverse, error, growth)
    factors, sides = split(inverse, 2), split(right, 2)
    out = dot3(factors, sides)
    rest = right - dot6(exact, split(out, 3))
    size = jnp.sum(rest * rest)
    out = out + dot3(factors, split(rest, 2))

    def slow():
        factors = split(invert(scaled, 0.1)[0], 2)
        return refine(exact, factors, right, scale, dot3(factors, sides))[1]

    return lax.cond(size <= 2e-5 * scale, lambda: out, slow) * down


def weights_of(refs):
    a1_ref, a2_ref, b1_ref, b2_ref, start_ref = refs
    a, b = a1_ref[...] + a2_ref[...], b1_ref[...] + b2_ref[...]
    return solve(unpack_gram(a), unpack_right(a, b), start_ref[...])


def shrink(data, low_rank, level):
    difference = data - low_rank
    size = jnp.maximum(jnp.abs(difference) - level, 0.0)
    return jnp.where(difference < 0, -size, size)


def middle_kernel(blocks, *refs):
    sum_refs, refs = refs[:5], refs[5:]
    left_top_ref, left_rest_ref, data_ref, level_ref, top_ref, rest_ref, *left_refs = refs
    tall = data_ref.shape[0] // blocks
    weights = split(weights_of(sum_refs), 2)
    left = []
    for p in range(blocks):
        at = pl.ds(p * tall, tall)
        low_rank = dot3((left_top_ref[at, :], left_rest_ref[at, :]), weights)
        data = data_ref[at, :]
        residual = split(data - shrink(data, low_rank, level_ref[...]), 2)
        top_ref[at, :], rest_ref[at, :] = residual
        left.append(dot3(residual, weights, NT))
    write_left(left, left_refs, blocks)


def last_kernel(blocks, *refs):
    sum_refs, refs = refs[:5], refs[5:]
    left_top_ref, left_rest_ref, data_ref, level_ref, low_rank_ref, sparse_ref, low_rank, sparse, sems = refs
    tall = data_ref.shape[0] // blocks
    low = lowest(blocks)
    weights = split(weights_of(sum_refs), 2)
    copies = []
    for p in range(blocks):
        at = pl.ds(p * tall, tall)
        low_rank[at, :] = dot3((left_top_ref[at, :], left_rest_ref[at, :]), weights)
        sparse[at, :] = shrink(data_ref[at, :], low_rank[at, :], level_ref[...])
        to = pl.ds(pl.multiple_of((p ^ low) * tall, tall), tall)
        for k, (source, target) in enumerate(((low_rank, low_rank_ref), (sparse, sparse_ref))):
            copies.append(pltpu.make_async_copy(source.at[at, :], target.at[to, :], sems.at[2 * p + k]))
            copies[-1].start()
    for copy in copies:
        copy.wait()


VMEM = pl.BlockSpec(memory_space=pltpu.VMEM)
HBM = pl.BlockSpec(memory_space=pltpu.HBM)


def call(body, args, outs, in_specs=None, out_specs=None, scratch=(), cost=None, name=None):
    return pl.pallas_call(
        body,
        out_shape=[jax.ShapeDtypeStruct(shape, dtype) for shape, dtype in outs],
        in_specs=in_specs or [VMEM] * len(args),
        out_specs=out_specs or [VMEM] * len(outs),
        scratch_shapes=list(scratch),
        compiler_params=pltpu.CompilerParams(vmem_limit_bytes=VMEM_BYTES),
        cost_estimate=cost,
        name=name,
    )(*args)


def per_device(n_tm, n_rows, snapshots, right_basis, threshold):
    rows, cols = snapshots.shape
    rank = right_basis.shape[1]
    blocks = n_tm // 2
    whole = [((rows, cols), bf16)] * 2
    a_rows = (rank + rank // 2 + SUBLANES) // 16 * 8 + SUBLANES
    lefts = [((rows // CHUNKS // 2, rank), f32)] * (2 * CHUNKS)
    data, top, rest, *left = call(
        functools.partial(head_kernel, blocks),
        (snapshots, right_basis),
        [((rows, cols), f32)] + whole + lefts,
        in_specs=[HBM] * 2,
        scratch=[
            pltpu.VMEM(right_basis.shape, f32),
            pltpu.SemaphoreType.DMA((blocks,)),
            pltpu.SemaphoreType.DMA,
        ],
        name="head",
    )
    level = threshold[None, :]
    for iteration in range(ITERS):
        pieces = sum_tm(list(zip(left[::2], left[1::2])), n_tm)
        a, b, left_top, left_rest = call(
            functools.partial(product_kernel, blocks, [len(x) for x in pieces]),
            (top, rest, *[x for parts in pieces for x in parts]),
            [((a_rows, cols), f32), ((rank + rank // 2 + SUBLANES - a_rows, cols), f32)] + [((rows, rank), bf16)] * 2,
            name="products",
        )
        sums = sum_rows(a, b, n_rows)
        start, level = call(
            inverse_kernel,
            (sums[0], level),
            [((rank, rank), f32), (level.shape, f32)],
            cost=pl.CostEstimate(flops=80 * rank**3, bytes_accessed=rank * rank * 8, transcendentals=0),
            name="inverse",
        )
        args = (*sums, start, left_top, left_rest, data, level)
        if iteration < ITERS - 1:
            top, rest, *left = call(
                functools.partial(middle_kernel, blocks),
                args,
                whole + lefts,
                name="middle",
            )
    return call(
        functools.partial(last_kernel, blocks),
        args,
        [((rows, cols), f32)] * 2,
        out_specs=[HBM] * 2,
        scratch=[pltpu.VMEM((rows, cols), f32)] * 2 + [pltpu.SemaphoreType.DMA((2 * blocks,))],
        name="last",
    )


def solution(mesh):
    return jax.shard_map(
        functools.partial(per_device, mesh.shape["tm"], mesh.shape["rows"]),
        mesh=mesh,
        in_specs=(P("rows", "tm"), P("tm", None), P("tm")),
        out_specs=(P("rows", "tm"), P("rows", "tm")),
        check_vma=False,
    )
```

```python
import functools
import jax
import jax.numpy as jnp
from jax import lax
from jax.experimental import pallas as pl
from jax.experimental.pallas import tpu as pltpu
from jax.sharding import PartitionSpec as P

ITERS = 2
SHARES = 6, 6, 4
SUBLANES = 8
LOW = 1e-3
NEAR, FAR = 1.25, 4.2
VMEM_BYTES = 16 << 20

NN = (((1,), (0,)), ((), ()))
NT = (((1,), (1,)), ((), ()))
TN = (((0,), (0,)), ((), ()))
f32, bf16 = jnp.float32, jnp.bfloat16


def split(x, terms):
    out = []
    for _ in range(terms):
        out.append(x.astype(bf16))
        x = x - out[-1].astype(f32)
    return out


def dot(a, b, dims=NN):
    return lax.dot_general(a, b, dims, preferred_element_type=f32)


def dot3(a, b, dims=NN):
    return dot(a[0], b[0], dims) + (dot(a[0], b[1], dims) + dot(a[1], b[0], dims))


def dot6(a, b):
    small = dot(a[0], b[2]) + dot(a[1], b[1]) + dot(a[2], b[0])
    return dot(a[0], b[0]) + (dot(a[0], b[1]) + dot(a[1], b[0]) + small)


def swap(x, axis, size, bit):
    return lax.ppermute(x, axis, [(i, i ^ bit) for i in range(size)])


def bits_of(size):
    return [1 << b for b in range(size.bit_length() - 1)]


def sum_tm(chunks, size):
    first, *middle, last = bits_of(size)
    chunks = [kept + swap(sent, "tm", size, first) for kept, sent in chunks]
    for bit in middle:
        for i, x in enumerate(chunks):
            half = x.shape[0] // 2
            chunks[i] = x[:half] + swap(x[half:], "tm", size, bit)
    pieces = []
    for x in chunks:
        x = x + swap(x, "tm", size, last)
        parts = [x]
        for bit in reversed(middle):
            x = parts[0] if len(parts) == 1 else jnp.concatenate(parts, 0)
            parts.append(swap(x, "tm", size, bit))
        pieces.append(parts + [swap(x, "tm", size, first) for x in parts])
    return pieces


def sum_rows(a, b, size):
    bits = bits_of(size)
    turn = len(bits) // 2
    pair_a, pair_b = None, None
    for bit_a, bit_b in zip(bits, bits[turn:] + bits[:turn]):
        a = a if pair_a is None else pair_a[0] + pair_a[1]
        b = b if pair_b is None else pair_b[0] + pair_b[1]
        pair_a, pair_b = (a, swap(a, "rows", size, bit_a)), (b, swap(b, "rows", size, bit_b))
    return pair_a + pair_b


def lowest(blocks):
    me = lax.axis_index("tm")
    low = 0
    for b in range(blocks.bit_length() - 1):
        low = low * 2 + lax.rem(me >> b, 2)
    return low


def chunks_of(tall):
    ends = [sum(SHARES[:i]) * tall // sum(SHARES) for i in range(len(SHARES) + 1)]
    return [(at, end - at) for at, end in zip(ends, ends[1:])]


def write_left(left, out_refs, blocks):
    for p in range(blocks):
        for c, (at, share) in enumerate(chunks_of(left[0].shape[0])):
            to = pl.ds(p % (blocks // 2) * share, share)
            out_refs[2 * c + p // (blocks // 2)][to, :] = left[p][at : at + share]


def fetches(snap_ref, data, sems, blocks):
    tall = data.shape[0] // blocks
    low = lowest(blocks)
    return [
        pltpu.make_async_copy(
            snap_ref.at[pl.ds(pl.multiple_of((p ^ low) * tall, tall), tall), :],
            data.at[pl.ds(p * tall, tall), :],
            sems.at[p],
        )
        for p in range(blocks)
    ]


def head_kernel(blocks, snap_ref, basis_ref, data, top_ref, rest_ref, *more):
    *left_refs, basis, sems, basis_sem = more
    tall = data.shape[0] // blocks
    copies = fetches(snap_ref, data, sems, blocks)
    first = pltpu.make_async_copy(basis_ref, basis, basis_sem)
    first.start()
    for copy in copies:
        copy.start()
    first.wait()
    basis = split(basis[...], 2)
    left = []
    for p in range(blocks):
        at = pl.ds(p * tall, tall)
        copies[p].wait()
        top_ref[at, :], rest_ref[at, :] = block = split(data[at, :], 2)
        left.append(dot3(block, basis))
    write_left(left, left_refs, blocks)


def product_kernel(blocks, counts, top_ref, rest_ref, *more):
    left_refs, (a_ref, b_ref, left_top_ref, left_rest_ref) = more[:-4], more[-4:]
    rows, rank = left_top_ref.shape
    tall = rows // blocks
    taken = 0
    for c, (at, share) in enumerate(chunks_of(tall)):
        p = 0
        for ref in left_refs[taken : taken + counts[c]]:
            terms = split(ref[...], 2)
            for k in range(ref.shape[0] // share):
                for out_ref, term in zip((left_top_ref, left_rest_ref), terms):
                    out_ref[pl.ds(p * tall + at, share), :] = term[k * share : (k + 1) * share]
                p += 1
        taken += counts[c]
    left = left_top_ref[...], left_rest_ref[...]
    right = dot3(left, (top_ref[...], rest_ref[...]), TN)
    cross = dot(left[0], left[1], TN)
    gram = dot(left[0], left[0], TN) + (cross + cross.T + dot(left[1], left[1], TN))
    pack(gram, right, a_ref, b_ref)


def pack(gram, right, a_ref, b_ref):
    half = gram.shape[0] // 2
    lower = below(half)
    a_ref[:half, :half] = jnp.where(lower, gram[:half, :half], gram[half:, half:])
    a_ref[:half, half:] = gram[half:, :half]
    diagonal = jnp.sum(jnp.where(identity(half), gram[half:, half:], 0.0), 0, keepdims=True)
    a_ref[half : half + SUBLANES, :] = jnp.broadcast_to(
        jnp.concatenate([diagonal, diagonal], 1), (SUBLANES, 2 * half)
    )
    taken = a_ref.shape[0] - half - SUBLANES
    a_ref[half + SUBLANES :, :] = right[:taken]
    b_ref[...] = right[taken:]


def unpack_gram(a):
    half = a.shape[1] // 2
    lower = below(half)
    both, off = a[:half, :half], a[:half, half:]
    turned = both.T
    first = jnp.where(lower, both, turned)
    second = jnp.where(identity(half), a[half : half + 1, :half], jnp.where(lower, turned, both))
    return jnp.concatenate([jnp.concatenate([first, off.T], 1), jnp.concatenate([off, second], 1)], 0)


def unpack_right(a, b):
    return jnp.concatenate([a[a.shape[1] // 2 + SUBLANES :], b], 0)


def identity(n):
    return lax.broadcasted_iota(jnp.int32, (n, n), 0) == lax.broadcasted_iota(jnp.int32, (n, n), 1)


def below(n):
    return lax.broadcasted_iota(jnp.int32, (n, n), 0) >= lax.broadcasted_iota(jnp.int32, (n, n), 1)


def norm_bound(x):
    return jnp.max(jnp.sum(jnp.abs(x), 0, keepdims=True))


def chebyshev(matrix, square, low, high):
    at_zero, slope = (high + low) / (high - low), 2.0 / (high - low)
    growth = 2.0 * at_zero * at_zero - 1.0
    a, b = 4.0 * at_zero * slope / growth, 2.0 * slope * slope / growth
    return a, b, identity(matrix.shape[0]).astype(f32) - a * matrix + b * square, growth


def double(inverse, error, growth):
    growth = 2.0 * growth * growth - 1.0
    eye = identity(error.shape[0]).astype(f32)
    terms = split(error, 2)
    inverse = (1.0 + 1.0 / growth) * (inverse + dot3(split(inverse, 2), terms))
    error = (1.0 + 1.0 / growth) * dot3(terms, terms) - (1.0 / growth) * eye
    return inverse, error, growth


def converge(inverse, error, growth, enough):
    def more(state):
        count, size, *_ = state
        return jnp.logical_and(count < 40, size > enough)

    def body(state):
        count, _, *state = state
        inverse, error, growth = double(*state)
        return count + 1, jnp.sum(state[1] * state[1]), inverse, error, jnp.minimum(growth, 1e4)

    _, size, inverse, *_ = lax.while_loop(more, body, (0, jnp.float32(1e9), inverse, error, growth))
    return inverse, size


def diagonals(gram):
    on_diag = jnp.where(identity(gram.shape[0]), gram, 0.0)
    return jnp.sum(on_diag, 1, keepdims=True), jnp.sum(on_diag, 0, keepdims=True)


def invert(scaled, enough):
    terms = split(scaled, 2)
    eye = identity(scaled.shape[0]).astype(f32)
    high = norm_bound(scaled)
    a, b, error, growth = chebyshev(scaled, dot3(terms, terms), LOW * high, high)
    return converge(a * eye - b * scaled, error, growth, enough)


def inverse_kernel(a_ref, level_ref, out_ref, level_out_ref):
    level_out_ref[...] = level_ref[...]
    gram = unpack_gram(a_ref[...])
    down, across = diagonals(gram)
    down, across = lax.rsqrt(down), lax.rsqrt(across)
    out_ref[...] = invert(gram * down * across, 0.5)[0] * down * across


def refine(exact, factors, right, scale, out):
    def again(state):
        count, size, _ = state
        return jnp.logical_and(count < 60, size > 2e-5 * scale)

    def body(state):
        count, _, out = state
        rest = right - dot6(exact, split(out, 3))
        return count + 1, jnp.sum(rest * rest), out + dot3(factors, split(rest, 2))

    return lax.while_loop(again, body, (0, 2.0 * scale, out))[1:]


def solve(gram, right, start):
    down, across = diagonals(gram)
    start = start * jnp.sqrt(down) * jnp.sqrt(across)
    down, across = lax.rsqrt(down), lax.rsqrt(across)
    scaled = gram * down * across
    right = right * down
    scale = jnp.sum(right * right)
    exact = split(scaled, 3)
    product = dot6(exact, split(start, 3))
    terms = split(product, 2)
    follow = dot3(split(start, 2), terms)
    a, b, error, growth = chebyshev(product, dot3(terms, terms), NEAR, FAR)
    inverse = a * start - b * follow
    while growth < 1e3:
        inverse, error, growth = double(inverse, error, growth)
    factors, sides = split(inverse, 2), split(right, 2)
    out = dot3(factors, sides)
    rest = right - dot6(exact, split(out, 3))
    size = jnp.sum(rest * rest)
    out = out + dot3(factors, split(rest, 2))

    def slow():
        factors = split(invert(scaled, 0.1)[0], 2)
        return refine(exact, factors, right, scale, dot3(factors, sides))[1]

    return lax.cond(size <= 2e-5 * scale, lambda: out, slow) * down


def weights_of(refs):
    a1_ref, a2_ref, b1_ref, b2_ref, start_ref = refs
    a, b = a1_ref[...] + a2_ref[...], b1_ref[...] + b2_ref[...]
    return solve(unpack_gram(a), unpack_right(a, b), start_ref[...])


def shrink(data, low_rank, level):
    difference = data - low_rank
    size = jnp.maximum(jnp.abs(difference) - level, 0.0)
    return jnp.where(difference < 0, -size, size)


def middle_kernel(blocks, *refs):
    sum_refs, refs = refs[:5], refs[5:]
    left_top_ref, left_rest_ref, data_ref, level_ref, top_ref, rest_ref, *left_refs = refs
    tall = data_ref.shape[0] // blocks
    weights = split(weights_of(sum_refs), 2)
    left = []
    for p in range(blocks):
        at = pl.ds(p * tall, tall)
        low_rank = dot3((left_top_ref[at, :], left_rest_ref[at, :]), weights)
        data = data_ref[at, :]
        residual = split(data - shrink(data, low_rank, level_ref[...]), 2)
        top_ref[at, :], rest_ref[at, :] = residual
        left.append(dot3(residual, weights, NT))
    write_left(left, left_refs, blocks)


def last_kernel(blocks, *refs):
    sum_refs, refs = refs[:5], refs[5:]
    left_top_ref, left_rest_ref, data_ref, level_ref, low_rank_ref, sparse_ref, low_rank, sparse, sems = refs
    tall = data_ref.shape[0] // blocks
    low = lowest(blocks)
    weights = split(weights_of(sum_refs), 2)
    copies = []
    for p in range(blocks):
        at = pl.ds(p * tall, tall)
        low_rank[at, :] = dot3((left_top_ref[at, :], left_rest_ref[at, :]), weights)
        sparse[at, :] = shrink(data_ref[at, :], low_rank[at, :], level_ref[...])
        to = pl.ds(pl.multiple_of((p ^ low) * tall, tall), tall)
        for k, (source, target) in enumerate(((low_rank, low_rank_ref), (sparse, sparse_ref))):
            copies.append(pltpu.make_async_copy(source.at[at, :], target.at[to, :], sems.at[2 * p + k]))
            copies[-1].start()
    for copy in copies:
        copy.wait()


VMEM = pl.BlockSpec(memory_space=pltpu.VMEM)
HBM = pl.BlockSpec(memory_space=pltpu.HBM)


def call(body, args, outs, in_specs=None, out_specs=None, scratch=(), cost=None, name=None):
    return pl.pallas_call(
        body,
        out_shape=[jax.ShapeDtypeStruct(shape, dtype) for shape, dtype in outs],
        in_specs=in_specs or [VMEM] * len(args),
        out_specs=out_specs or [VMEM] * len(outs),
        scratch_shapes=list(scratch),
        compiler_params=pltpu.CompilerParams(vmem_limit_bytes=VMEM_BYTES),
        cost_estimate=cost,
        name=name,
    )(*args)


def per_device(n_tm, n_rows, snapshots, right_basis, threshold):
    rows, cols = snapshots.shape
    rank = right_basis.shape[1]
    blocks = n_tm // 2
    whole = [((rows, cols), bf16)] * 2
    a_rows = (rank + rank // 2 + SUBLANES) // 16 * 8 + SUBLANES
    lefts = [((share * blocks // 2, rank), f32) for _, share in chunks_of(rows // blocks) for _ in range(2)]
    data, top, rest, *left = call(
        functools.partial(head_kernel, blocks),
        [pltpu.with_memory_space_constraint(x, pltpu.HBM) for x in (snapshots, right_basis)],
        [((rows, cols), f32)] + whole + lefts,
        in_specs=[HBM] * 2,
        scratch=[
            pltpu.VMEM(right_basis.shape, f32),
            pltpu.SemaphoreType.DMA((blocks,)),
            pltpu.SemaphoreType.DMA,
        ],
        name="head",
    )
    level = threshold[None, :]
    for iteration in range(ITERS):
        pieces = sum_tm(list(zip(left[::2], left[1::2])), n_tm)
        a, b, left_top, left_rest = call(
            functools.partial(product_kernel, blocks, [len(x) for x in pieces]),
            (top, rest, *[x for parts in pieces for x in parts]),
            [((a_rows, cols), f32), ((rank + rank // 2 + SUBLANES - a_rows, cols), f32)] + [((rows, rank), bf16)] * 2,
            name="products",
        )
        sums = sum_rows(a, b, n_rows)
        start, level = call(
            inverse_kernel,
            (sums[0], level),
            [((rank, rank), f32), (level.shape, f32)],
            cost=pl.CostEstimate(flops=80 * rank**3, bytes_accessed=rank * rank * 8, transcendentals=0),
            name="inverse",
        )
        args = (*sums, start, left_top, left_rest, data, level)
        if iteration < ITERS - 1:
            top, rest, *left = call(
                functools.partial(middle_kernel, blocks),
                args,
                whole + lefts,
                name="middle",
            )
    return call(
        functools.partial(last_kernel, blocks),
        args,
        [((rows, cols), f32)] * 2,
        out_specs=[HBM] * 2,
        scratch=[pltpu.VMEM((rows, cols), f32)] * 2 + [pltpu.SemaphoreType.DMA((2 * blocks,))],
        name="last",
    )


def solution(mesh):
    return jax.shard_map(
        functools.partial(per_device, mesh.shape["tm"], mesh.shape["rows"]),
        mesh=mesh,
        in_specs=(P("rows", "tm"), P("tm", None), P("tm")),
        out_specs=(P("rows", "tm"), P("rows", "tm")),
        check_vma=False,
    )
```

```python
import functools
import jax
import jax.numpy as jnp
from jax import lax
from jax.experimental import pallas as pl
from jax.experimental.pallas import tpu as pltpu
from jax.sharding import PartitionSpec as P

ITERS = 2
SHARES = 6, 6, 4
SUBLANES = 8
LOW = 7e-4
NEAR, FAR = 1.25, 4.2
VMEM_BYTES = 16 << 20

NN = (((1,), (0,)), ((), ()))
NT = (((1,), (1,)), ((), ()))
TN = (((0,), (0,)), ((), ()))
f32, bf16 = jnp.float32, jnp.bfloat16


def split(x, terms):
    out = []
    for _ in range(terms):
        out.append(x.astype(bf16))
        x = x - out[-1].astype(f32)
    return out


def dot(a, b, dims=NN):
    return lax.dot_general(a, b, dims, preferred_element_type=f32)


def dot3(a, b, dims=NN):
    return dot(a[0], b[0], dims) + (dot(a[0], b[1], dims) + dot(a[1], b[0], dims))


def dot6(a, b):
    small = dot(a[0], b[2]) + dot(a[1], b[1]) + dot(a[2], b[0])
    return dot(a[0], b[0]) + (dot(a[0], b[1]) + dot(a[1], b[0]) + small)


def swap(x, axis, size, bit):
    return lax.ppermute(x, axis, [(i, i ^ bit) for i in range(size)])


def bits_of(size):
    return [1 << b for b in range(size.bit_length() - 1)]


def sum_tm(chunks, size):
    first, *middle, last = bits_of(size)
    chunks = [kept + swap(sent, "tm", size, first) for kept, sent in chunks]
    for bit in middle:
        for i, x in enumerate(chunks):
            half = x.shape[0] // 2
            chunks[i] = x[:half] + swap(x[half:], "tm", size, bit)
    pieces = []
    for x in chunks:
        x = x + swap(x, "tm", size, last)
        parts = [x]
        for bit in reversed(middle):
            x = parts[0] if len(parts) == 1 else jnp.concatenate(parts, 0)
            parts.append(swap(x, "tm", size, bit))
        pieces.append(parts + [swap(x, "tm", size, first) for x in parts])
    return pieces


def sum_rows(parts, turns, size):
    bits = bits_of(size)
    out = []
    for x, turn in zip(parts, turns):
        order = bits[turn * (len(bits) // 2) :] + bits[: turn * (len(bits) // 2)]
        for bit in order[:-1]:
            x = x + swap(x, "rows", size, bit)
        out += [x, swap(x, "rows", size, order[-1])]
    return out


def lowest(blocks):
    me = lax.axis_index("tm")
    low = 0
    for b in range(blocks.bit_length() - 1):
        low = low * 2 + lax.rem(me >> b, 2)
    return low


def chunks_of(tall):
    ends = [(sum(SHARES[:i]) * tall // sum(SHARES) + 8) // 16 * 16 for i in range(len(SHARES) + 1)]
    return [(at, end - at) for at, end in zip(ends, ends[1:])]


def write_left(left, out_refs, blocks):
    for p in range(blocks):
        for c, (at, share) in enumerate(chunks_of(left[0].shape[0])):
            to = pl.ds(p % (blocks // 2) * share, share)
            out_refs[2 * c + p // (blocks // 2)][to, :] = left[p][at : at + share]


def fetches(snap_ref, data, sems, blocks):
    tall = data.shape[0] // blocks
    low = lowest(blocks)
    return [
        pltpu.make_async_copy(
            snap_ref.at[pl.ds(pl.multiple_of((p ^ low) * tall, tall), tall), :],
            data.at[pl.ds(p * tall, tall), :],
            sems.at[p],
        )
        for p in range(blocks)
    ]


def head_kernel(blocks, snap_ref, basis_ref, data, top_ref, rest_ref, *more):
    *left_refs, basis, sems, basis_sem = more
    tall = data.shape[0] // blocks
    copies = fetches(snap_ref, data, sems, blocks)
    first = pltpu.make_async_copy(basis_ref, basis, basis_sem)
    first.start()
    for copy in copies:
        copy.start()
    first.wait()
    basis = split(basis[...], 2)
    left = []
    for p in range(blocks):
        at = pl.ds(p * tall, tall)
        copies[p].wait()
        top_ref[at, :], rest_ref[at, :] = block = split(data[at, :], 2)
        left.append(dot3(block, basis))
    write_left(left, left_refs, blocks)


def gram_kernel(blocks, counts, *more):
    left_refs, (gram_ref, left_top_ref, left_rest_ref) = more[:-3], more[-3:]
    rows, rank = left_top_ref.shape
    tall = rows // blocks
    taken = 0
    for c, (at, share) in enumerate(chunks_of(tall)):
        p = 0
        for ref in left_refs[taken : taken + counts[c]]:
            terms = split(ref[...], 2)
            for k in range(ref.shape[0] // share):
                for out_ref, term in zip((left_top_ref, left_rest_ref), terms):
                    out_ref[pl.ds(p * tall + at, share), :] = term[k * share : (k + 1) * share]
                p += 1
        taken += counts[c]
    left = left_top_ref[...], left_rest_ref[...]
    cross = dot(left[0], left[1], TN)
    gram = dot(left[0], left[0], TN) + (cross + cross.T + dot(left[1], left[1], TN))
    pack(gram, gram_ref)


def right_kernel(left_top_ref, left_rest_ref, top_ref, rest_ref, a_ref, b_ref):
    right = dot3((left_top_ref[...], left_rest_ref[...]), (top_ref[...], rest_ref[...]), TN)
    a_ref[...], b_ref[...] = right[: a_ref.shape[0]], right[a_ref.shape[0] :]


def pack(gram, out_ref):
    half = gram.shape[0] // 2
    out_ref[:half, :half] = jnp.where(below(half), gram[:half, :half], gram[half:, half:])
    out_ref[:half, half:] = gram[half:, :half]
    diagonal = jnp.sum(jnp.where(identity(half), gram[half:, half:], 0.0), 0, keepdims=True)
    out_ref[half:, :] = jnp.broadcast_to(jnp.concatenate([diagonal, diagonal], 1), (SUBLANES, 2 * half))


def unpack_gram(a):
    half = a.shape[1] // 2
    lower = below(half)
    both, off = a[:half, :half], a[:half, half:]
    turned = both.T
    first = jnp.where(lower, both, turned)
    second = jnp.where(identity(half), a[half : half + 1, :half], jnp.where(lower, turned, both))
    return jnp.concatenate([jnp.concatenate([first, off.T], 1), jnp.concatenate([off, second], 1)], 0)


def identity(n):
    return lax.broadcasted_iota(jnp.int32, (n, n), 0) == lax.broadcasted_iota(jnp.int32, (n, n), 1)


def below(n):
    return lax.broadcasted_iota(jnp.int32, (n, n), 0) >= lax.broadcasted_iota(jnp.int32, (n, n), 1)


def norm_bound(x):
    return jnp.max(jnp.sum(jnp.abs(x), 0, keepdims=True))


def chebyshev(matrix, square, low, high):
    at_zero, slope = (high + low) / (high - low), 2.0 / (high - low)
    growth = 2.0 * at_zero * at_zero - 1.0
    a, b = 4.0 * at_zero * slope / growth, 2.0 * slope * slope / growth
    return a, b, identity(matrix.shape[0]).astype(f32) - a * matrix + b * square, growth


def double(inverse, error, growth):
    growth = 2.0 * growth * growth - 1.0
    eye = identity(error.shape[0]).astype(f32)
    terms = split(error, 2)
    inverse = (1.0 + 1.0 / growth) * (inverse + dot3(split(inverse, 2), terms))
    error = (1.0 + 1.0 / growth) * dot3(terms, terms) - (1.0 / growth) * eye
    return inverse, error, growth


def converge(inverse, error, growth, enough):
    def more(state):
        count, size, *_ = state
        return jnp.logical_and(count < 40, size > enough)

    def body(state):
        count, _, *state = state
        inverse, error, growth = double(*state)
        return count + 1, jnp.sum(state[1] * state[1]), inverse, error, jnp.minimum(growth, 1e4)

    _, size, inverse, *_ = lax.while_loop(more, body, (0, jnp.float32(1e9), inverse, error, growth))
    return inverse, size


def diagonals(gram):
    on_diag = jnp.where(identity(gram.shape[0]), gram, 0.0)
    return jnp.sum(on_diag, 1, keepdims=True), jnp.sum(on_diag, 0, keepdims=True)


def begin(scaled):
    terms = split(scaled, 2)
    eye = identity(scaled.shape[0]).astype(f32)
    high = norm_bound(scaled)
    step = 1.0 / high
    a, b, error, growth = chebyshev(step * scaled, (step * step) * dot3(terms, terms), LOW, 1.0)
    return step * (a * eye - (b * step) * scaled), error, growth


def invert(scaled, enough):
    inverse, error, growth = begin(scaled)
    return converge(inverse, error, jnp.float32(growth), enough)


def inverse_kernel(a_ref, level_ref, out_ref, level_out_ref):
    level_out_ref[...] = level_ref[...]
    gram = unpack_gram(a_ref[...])
    down, across = diagonals(gram)
    down, across = lax.rsqrt(down), lax.rsqrt(across)
    inverse, error, growth = begin(gram * down * across)
    while growth < 10.0:
        inverse, error, growth = double(inverse, error, growth)
    out_ref[...] = inverse * down * across


def refine(exact, factors, right, scale, out):
    def again(state):
        count, size, _ = state
        return jnp.logical_and(count < 60, size > 2e-5 * scale)

    def body(state):
        count, _, out = state
        rest = right - dot6(exact, split(out, 3))
        return count + 1, jnp.sum(rest * rest), out + dot3(factors, split(rest, 2))

    return lax.while_loop(again, body, (0, 2.0 * scale, out))[1:]


def prepare_kernel(half_ref, other_ref, start_ref, top_ref, rest_ref, *out_refs):
    gram = unpack_gram(half_ref[...] + other_ref[...])
    down, across = diagonals(gram)
    start = start_ref[...] * jnp.sqrt(down) * jnp.sqrt(across)
    down, across = lax.rsqrt(down), lax.rsqrt(across)
    exact = split(gram * down * across, 3)
    product = dot6(exact, split(start, 3))
    terms = split(product, 2)
    follow = dot3(split(start, 2), terms)
    a, b, error, growth = chebyshev(product, dot3(terms, terms), NEAR, FAR)
    inverse = a * start - b * follow
    while growth < 1e3:
        inverse, error, growth = double(inverse, error, growth)
    top_ref[...], rest_ref[...] = split(inverse, 2)
    *exact_refs, down_ref = out_refs
    for ref, term in zip(exact_refs, exact):
        ref[...] = term
    down_ref[...] = jnp.broadcast_to(down, down_ref.shape)


def weights_of(refs):
    a_ref, other_a_ref, b_ref, other_b_ref, top_ref, rest_ref, *exact_refs, down_ref = refs
    down = down_ref[:, :1]
    right = jnp.concatenate([a_ref[...] + other_a_ref[...], b_ref[...] + other_b_ref[...]], 0) * down
    factors, exact = (top_ref[...], rest_ref[...]), [ref[...] for ref in exact_refs]
    scale = jnp.sum(right * right)
    sides = split(right, 2)
    out = dot3(factors, sides)
    rest = right - dot6(exact, split(out, 3))
    size = jnp.sum(rest * rest)
    out = out + dot3(factors, split(rest, 2))

    def slow():
        scaled = exact[0].astype(f32) + (exact[1].astype(f32) + exact[2].astype(f32))
        factors = split(invert(scaled, 0.1)[0], 2)
        return refine(exact, factors, right, scale, dot3(factors, sides))[1]

    return lax.cond(size <= 2e-5 * scale, lambda: out, slow) * down


def shrink(data, low_rank, level):
    difference = data - low_rank
    size = jnp.maximum(jnp.abs(difference) - level, 0.0)
    return jnp.where(difference < 0, -size, size)


def middle_kernel(blocks, *refs):
    sum_refs, refs = refs[:10], refs[10:]
    left_top_ref, left_rest_ref, data_ref, level_ref, top_ref, rest_ref, *left_refs = refs
    tall = data_ref.shape[0] // blocks
    weights = split(weights_of(sum_refs), 2)
    left = []
    for p in range(blocks):
        at = pl.ds(p * tall, tall)
        low_rank = dot3((left_top_ref[at, :], left_rest_ref[at, :]), weights)
        data = data_ref[at, :]
        residual = split(data - shrink(data, low_rank, level_ref[...]), 2)
        top_ref[at, :], rest_ref[at, :] = residual
        left.append(dot3(residual, weights, NT))
    write_left(left, left_refs, blocks)


def last_kernel(blocks, *refs):
    sum_refs, refs = refs[:10], refs[10:]
    left_top_ref, left_rest_ref, data_ref, level_ref, low_rank_ref, sparse_ref, low_rank, sparse, sems = refs
    tall = data_ref.shape[0] // blocks
    low = lowest(blocks)
    weights = split(weights_of(sum_refs), 2)
    copies = []
    for p in range(blocks):
        at = pl.ds(p * tall, tall)
        low_rank[at, :] = dot3((left_top_ref[at, :], left_rest_ref[at, :]), weights)
        sparse[at, :] = shrink(data_ref[at, :], low_rank[at, :], level_ref[...])
        to = pl.ds(pl.multiple_of((p ^ low) * tall, tall), tall)
        for k, (source, target) in enumerate(((low_rank, low_rank_ref), (sparse, sparse_ref))):
            copies.append(pltpu.make_async_copy(source.at[at, :], target.at[to, :], sems.at[2 * p + k]))
            copies[-1].start()
    for copy in copies:
        copy.wait()


VMEM = pl.BlockSpec(memory_space=pltpu.VMEM)
HBM = pl.BlockSpec(memory_space=pltpu.HBM)


def call(body, args, outs, in_specs=None, out_specs=None, scratch=(), cost=None, name=None):
    return pl.pallas_call(
        body,
        out_shape=[jax.ShapeDtypeStruct(shape, dtype) for shape, dtype in outs],
        in_specs=in_specs or [VMEM] * len(args),
        out_specs=out_specs or [VMEM] * len(outs),
        scratch_shapes=list(scratch),
        compiler_params=pltpu.CompilerParams(vmem_limit_bytes=VMEM_BYTES),
        cost_estimate=cost,
        name=name,
    )(*args)


def per_device(n_tm, n_rows, snapshots, right_basis, threshold):
    rows, cols = snapshots.shape
    rank = right_basis.shape[1]
    blocks = n_tm // 2
    whole = [((rows, cols), bf16)] * 2
    lefts = [((share * blocks // 2, rank), f32) for _, share in chunks_of(rows // blocks) for _ in range(2)]
    data, top, rest, *left = call(
        functools.partial(head_kernel, blocks),
        [pltpu.with_memory_space_constraint(x, pltpu.HBM) for x in (snapshots, right_basis)],
        [((rows, cols), f32)] + whole + lefts,
        in_specs=[HBM] * 2,
        scratch=[
            pltpu.VMEM(right_basis.shape, f32),
            pltpu.SemaphoreType.DMA((blocks,)),
            pltpu.SemaphoreType.DMA,
        ],
        name="head",
    )
    level = threshold[None, :]
    for iteration in range(ITERS):
        pieces = sum_tm(list(zip(left[::2], left[1::2])), n_tm)
        gram, left_top, left_rest = call(
            functools.partial(gram_kernel, blocks, [len(x) for x in pieces]),
            [x for parts in pieces for x in parts],
            [((rank // 2 + SUBLANES, rank), f32)] + [((rows, rank), bf16)] * 2,
            name="gram",
        )
        a, b = call(
            right_kernel,
            (left_top, left_rest, top, rest),
            [((rank // 4, cols), f32), ((rank - rank // 4, cols), f32)],
            name="right",
        )
        gram, other_gram, *sums = sum_rows((gram, a, b), (0, 0, 1), n_rows)
        start, level = call(
            inverse_kernel,
            (gram, level),
            [((rank, rank), f32), (level.shape, f32)],
            cost=pl.CostEstimate(flops=80 * rank**3, bytes_accessed=rank * rank * 8, transcendentals=0),
            name="inverse",
        )
        prepared = call(
            prepare_kernel,
            (gram, other_gram, start),
            [((rank, rank), bf16)] * 5 + [((rank, 128), f32)],
            cost=pl.CostEstimate(flops=60 * rank**3, bytes_accessed=rank * rank * 8, transcendentals=0),
            name="prepare",
        )
        args = (*sums, *prepared, left_top, left_rest, data, level)
        if iteration < ITERS - 1:
            top, rest, *left = call(
                functools.partial(middle_kernel, blocks),
                args,
                whole + lefts,
                name="middle",
            )
    return call(
        functools.partial(last_kernel, blocks),
        args,
        [((rows, cols), f32)] * 2,
        out_specs=[HBM] * 2,
        scratch=[pltpu.VMEM((rows, cols), f32)] * 2 + [pltpu.SemaphoreType.DMA((2 * blocks,))],
        name="last",
    )


def solution(mesh):
    return jax.shard_map(
        functools.partial(per_device, mesh.shape["tm"], mesh.shape["rows"]),
        mesh=mesh,
        in_specs=(P("rows", "tm"), P("tm", None), P("tm")),
        out_specs=(P("rows", "tm"), P("rows", "tm")),
        check_vma=False,
    )
```

```python
import functools
import jax
import jax.numpy as jnp
from jax import lax
from jax.experimental import pallas as pl
from jax.experimental.pallas import tpu as pltpu
from jax.sharding import PartitionSpec as P

ITERS = 2
SHARES = 6, 6, 4
SUBLANES = 8
LOW = 7e-4
NEAR, FAR = 1.25, 4.2
VMEM_BYTES = 16 << 20

NN = (((1,), (0,)), ((), ()))
NT = (((1,), (1,)), ((), ()))
TN = (((0,), (0,)), ((), ()))
f32, bf16 = jnp.float32, jnp.bfloat16


def split(x, terms):
    out = []
    for _ in range(terms):
        out.append(x.astype(bf16))
        x = x - out[-1].astype(f32)
    return out


def dot(a, b, dims=NN):
    return lax.dot_general(a, b, dims, preferred_element_type=f32)


def dot3(a, b, dims=NN):
    return dot(a[0], b[0], dims) + (dot(a[0], b[1], dims) + dot(a[1], b[0], dims))


def dot6(a, b):
    small = dot(a[0], b[2]) + dot(a[1], b[1]) + dot(a[2], b[0])
    return dot(a[0], b[0]) + (dot(a[0], b[1]) + dot(a[1], b[0]) + small)


def swap(x, axis, size, bit):
    return lax.ppermute(x, axis, [(i, i ^ bit) for i in range(size)])


def bits_of(size):
    return [1 << b for b in range(size.bit_length() - 1)]


def sum_tm(chunks, size):
    first, *middle, last = bits_of(size)
    chunks = [kept + swap(sent, "tm", size, first) for kept, sent in chunks]
    for bit in middle:
        for i, x in enumerate(chunks):
            half = x.shape[0] // 2
            chunks[i] = x[:half] + swap(x[half:], "tm", size, bit)
    pieces = []
    for x in chunks:
        x = x + swap(x, "tm", size, last)
        parts = [x]
        for bit in reversed(middle):
            x = parts[0] if len(parts) == 1 else jnp.concatenate(parts, 0)
            parts.append(swap(x, "tm", size, bit))
        pieces.append(parts + [swap(x, "tm", size, first) for x in parts])
    return pieces


def sum_rows(parts, turns, size):
    bits = bits_of(size)
    out = []
    for x, turn in zip(parts, turns):
        order = bits[turn * (len(bits) // 2) :] + bits[: turn * (len(bits) // 2)]
        for bit in order[:-1]:
            x = x + swap(x, "rows", size, bit)
        out += [x, swap(x, "rows", size, order[-1])]
    return out


def lowest(blocks):
    me = lax.axis_index("tm")
    low = 0
    for b in range(blocks.bit_length() - 1):
        low = low * 2 + lax.rem(me >> b, 2)
    return low


def chunks_of(tall):
    ends = [(sum(SHARES[:i]) * tall // sum(SHARES) + 8) // 16 * 16 for i in range(len(SHARES) + 1)]
    return [(at, end - at) for at, end in zip(ends, ends[1:])]


def write_left(left, out_refs, blocks):
    for p in range(blocks):
        for c, (at, share) in enumerate(chunks_of(left[0].shape[0])):
            to = pl.ds(p % (blocks // 2) * share, share)
            out_refs[2 * c + p // (blocks // 2)][to, :] = left[p][at : at + share]


def fetches(snap_ref, data, sems, blocks):
    tall = data.shape[0] // blocks
    low = lowest(blocks)
    return [
        pltpu.make_async_copy(
            snap_ref.at[pl.ds(pl.multiple_of((p ^ low) * tall, tall), tall), :],
            data.at[pl.ds(p * tall, tall), :],
            sems.at[p],
        )
        for p in range(blocks)
    ]


def head_kernel(blocks, snap_ref, basis_ref, data, top_ref, rest_ref, *more):
    *left_refs, basis, sems, basis_sem = more
    tall = data.shape[0] // blocks
    copies = fetches(snap_ref, data, sems, blocks)
    first = pltpu.make_async_copy(basis_ref, basis, basis_sem)
    first.start()
    for copy in copies:
        copy.start()
    first.wait()
    basis = split(basis[...], 2)
    left = []
    for p in range(blocks):
        at = pl.ds(p * tall, tall)
        copies[p].wait()
        top_ref[at, :], rest_ref[at, :] = block = split(data[at, :], 2)
        left.append(dot3(block, basis))
    write_left(left, left_refs, blocks)


def product_kernel(blocks, counts, top_ref, rest_ref, *more):
    left_refs, (first_ref, second_ref, left_top_ref, left_rest_ref) = more[:-4], more[-4:]
    rows, rank = left_top_ref.shape
    tall = rows // blocks
    taken = 0
    for c, (at, share) in enumerate(chunks_of(tall)):
        p = 0
        for ref in left_refs[taken : taken + counts[c]]:
            terms = split(ref[...], 2)
            for k in range(ref.shape[0] // share):
                for out_ref, term in zip((left_top_ref, left_rest_ref), terms):
                    out_ref[pl.ds(p * tall + at, share), :] = term[k * share : (k + 1) * share]
                p += 1
        taken += counts[c]
    left = left_top_ref[...], left_rest_ref[...]
    right = dot3(left, (top_ref[...], rest_ref[...]), TN)
    head = rank // 2 + SUBLANES
    taken = first_ref.shape[0] - head
    first_ref[head:, :], second_ref[...] = right[:taken], right[taken:]
    cross = dot(left[0], left[1], TN)
    gram = dot(left[0], left[0], TN) + (cross + cross.T + dot(left[1], left[1], TN))
    pack(gram, first_ref)


def pack(gram, out_ref):
    half = gram.shape[0] // 2
    out_ref[:half, :half] = jnp.where(below(half), gram[:half, :half], gram[half:, half:])
    out_ref[:half, half:] = gram[half:, :half]
    diagonal = jnp.sum(jnp.where(identity(half), gram[half:, half:], 0.0), 0, keepdims=True)
    out_ref[half : half + SUBLANES, :] = jnp.broadcast_to(jnp.concatenate([diagonal, diagonal], 1), (SUBLANES, 2 * half))


def unpack_gram(a):
    half = a.shape[1] // 2
    lower = below(half)
    both, off = a[:half, :half], a[:half, half:]
    turned = both.T
    first = jnp.where(lower, both, turned)
    second = jnp.where(identity(half), a[half : half + 1, :half], jnp.where(lower, turned, both))
    return jnp.concatenate([jnp.concatenate([first, off.T], 1), jnp.concatenate([off, second], 1)], 0)


def identity(n):
    return lax.broadcasted_iota(jnp.int32, (n, n), 0) == lax.broadcasted_iota(jnp.int32, (n, n), 1)


def below(n):
    return lax.broadcasted_iota(jnp.int32, (n, n), 0) >= lax.broadcasted_iota(jnp.int32, (n, n), 1)


def norm_bound(x):
    return jnp.max(jnp.sum(jnp.abs(x), 0, keepdims=True))


def chebyshev(matrix, square, low, high):
    at_zero, slope = (high + low) / (high - low), 2.0 / (high - low)
    growth = 2.0 * at_zero * at_zero - 1.0
    a, b = 4.0 * at_zero * slope / growth, 2.0 * slope * slope / growth
    return a, b, identity(matrix.shape[0]).astype(f32) - a * matrix + b * square, growth


def double(inverse, error, growth):
    growth = 2.0 * growth * growth - 1.0
    eye = identity(error.shape[0]).astype(f32)
    terms = split(error, 2)
    inverse = (1.0 + 1.0 / growth) * (inverse + dot3(split(inverse, 2), terms))
    error = (1.0 + 1.0 / growth) * dot3(terms, terms) - (1.0 / growth) * eye
    return inverse, error, growth


def converge(inverse, error, growth, enough):
    def more(state):
        count, size, *_ = state
        return jnp.logical_and(count < 40, size > enough)

    def body(state):
        count, _, *state = state
        inverse, error, growth = double(*state)
        return count + 1, jnp.sum(state[1] * state[1]), inverse, error, jnp.minimum(growth, 1e4)

    _, size, inverse, *_ = lax.while_loop(more, body, (0, jnp.float32(1e9), inverse, error, growth))
    return inverse, size


def diagonals(gram):
    on_diag = jnp.where(identity(gram.shape[0]), gram, 0.0)
    return jnp.sum(on_diag, 1, keepdims=True), jnp.sum(on_diag, 0, keepdims=True)


def begin(scaled):
    terms = split(scaled, 2)
    eye = identity(scaled.shape[0]).astype(f32)
    high = norm_bound(scaled)
    step = 1.0 / high
    a, b, error, growth = chebyshev(step * scaled, (step * step) * dot3(terms, terms), LOW, 1.0)
    return step * (a * eye - (b * step) * scaled), error, growth


def invert(scaled, enough):
    inverse, error, growth = begin(scaled)
    return converge(inverse, error, jnp.float32(growth), enough)


def inverse_kernel(a_ref, level_ref, out_ref, level_out_ref):
    level_out_ref[...] = level_ref[...]
    gram = unpack_gram(a_ref[...])
    down, across = diagonals(gram)
    down, across = lax.rsqrt(down), lax.rsqrt(across)
    inverse, error, growth = begin(gram * down * across)
    while growth < 10.0:
        inverse, error, growth = double(inverse, error, growth)
    out_ref[...] = inverse * down * across


def refine(exact, factors, right, scale, out):
    def again(state):
        count, size, _ = state
        return jnp.logical_and(count < 60, size > 2e-5 * scale)

    def body(state):
        count, _, out = state
        rest = right - dot6(exact, split(out, 3))
        return count + 1, jnp.sum(rest * rest), out + dot3(factors, split(rest, 2))

    return lax.while_loop(again, body, (0, 2.0 * scale, out))[1:]


def prepare_kernel(half_ref, other_ref, start_ref, top_ref, rest_ref, *out_refs):
    gram = unpack_gram(half_ref[...] + other_ref[...])
    down, across = diagonals(gram)
    start = start_ref[...] * jnp.sqrt(down) * jnp.sqrt(across)
    down, across = lax.rsqrt(down), lax.rsqrt(across)
    exact = split(gram * down * across, 3)
    product = dot6(exact, split(start, 3))
    terms = split(product, 2)
    follow = dot3(split(start, 2), terms)
    a, b, error, growth = chebyshev(product, dot3(terms, terms), NEAR, FAR)
    inverse = a * start - b * follow
    while growth < 1e3:
        inverse, error, growth = double(inverse, error, growth)
    top_ref[...], rest_ref[...] = split(inverse, 2)
    *exact_refs, down_ref = out_refs
    for ref, term in zip(exact_refs, exact):
        ref[...] = term
    down_ref[...] = jnp.broadcast_to(down, down_ref.shape)


def weights_of(refs):
    first_ref, other_first_ref, second_ref, other_second_ref, top_ref, rest_ref, *exact_refs, down_ref = refs
    head = first_ref.shape[1] // 2 + SUBLANES
    down = down_ref[:, :1]
    right = jnp.concatenate([first_ref[head:, :] + other_first_ref[head:, :], second_ref[...] + other_second_ref[...]], 0) * down
    factors, exact = (top_ref[...], rest_ref[...]), [ref[...] for ref in exact_refs]
    scale = jnp.sum(right * right)
    sides = split(right, 2)
    out = dot3(factors, sides)
    rest = right - dot6(exact, split(out, 3))
    size = jnp.sum(rest * rest)
    out = out + dot3(factors, split(rest, 2))

    def slow():
        scaled = exact[0].astype(f32) + (exact[1].astype(f32) + exact[2].astype(f32))
        factors = split(invert(scaled, 0.1)[0], 2)
        return refine(exact, factors, right, scale, dot3(factors, sides))[1]

    return lax.cond(size <= 2e-5 * scale, lambda: out, slow) * down


def shrink(data, low_rank, level):
    difference = data - low_rank
    size = jnp.maximum(jnp.abs(difference) - level, 0.0)
    return jnp.where(difference < 0, -size, size)


def middle_kernel(blocks, *refs):
    sum_refs, refs = refs[:10], refs[10:]
    left_top_ref, left_rest_ref, data_ref, level_ref, top_ref, rest_ref, *left_refs = refs
    tall = data_ref.shape[0] // blocks
    weights = split(weights_of(sum_refs), 2)
    left = []
    for p in range(blocks):
        at = pl.ds(p * tall, tall)
        low_rank = dot3((left_top_ref[at, :], left_rest_ref[at, :]), weights)
        data = data_ref[at, :]
        residual = split(data - shrink(data, low_rank, level_ref[...]), 2)
        top_ref[at, :], rest_ref[at, :] = residual
        left.append(dot3(residual, weights, NT))
    write_left(left, left_refs, blocks)


def last_kernel(blocks, *refs):
    sum_refs, refs = refs[:10], refs[10:]
    left_top_ref, left_rest_ref, data_ref, level_ref, low_rank_ref, sparse_ref, low_rank, sparse, sems = refs
    tall = data_ref.shape[0] // blocks
    low = lowest(blocks)
    weights = split(weights_of(sum_refs), 2)
    copies = []
    for p in range(blocks):
        at = pl.ds(p * tall, tall)
        low_rank[at, :] = dot3((left_top_ref[at, :], left_rest_ref[at, :]), weights)
        sparse[at, :] = shrink(data_ref[at, :], low_rank[at, :], level_ref[...])
        to = pl.ds(pl.multiple_of((p ^ low) * tall, tall), tall)
        for k, (source, target) in enumerate(((low_rank, low_rank_ref), (sparse, sparse_ref))):
            copies.append(pltpu.make_async_copy(source.at[at, :], target.at[to, :], sems.at[2 * p + k]))
            copies[-1].start()
    for copy in copies:
        copy.wait()


VMEM = pl.BlockSpec(memory_space=pltpu.VMEM)
HBM = pl.BlockSpec(memory_space=pltpu.HBM)


def call(body, args, outs, in_specs=None, out_specs=None, scratch=(), cost=None, name=None):
    return pl.pallas_call(
        body,
        out_shape=[jax.ShapeDtypeStruct(shape, dtype) for shape, dtype in outs],
        in_specs=in_specs or [VMEM] * len(args),
        out_specs=out_specs or [VMEM] * len(outs),
        scratch_shapes=list(scratch),
        compiler_params=pltpu.CompilerParams(vmem_limit_bytes=VMEM_BYTES),
        cost_estimate=cost,
        name=name,
    )(*args)


def per_device(n_tm, n_rows, snapshots, right_basis, threshold):
    rows, cols = snapshots.shape
    rank = right_basis.shape[1]
    blocks = n_tm // 2
    whole = [((rows, cols), bf16)] * 2
    first_rows = rank // 2 + SUBLANES + rank // 8
    lefts = [((share * blocks // 2, rank), f32) for _, share in chunks_of(rows // blocks) for _ in range(2)]
    data, top, rest, *left = call(
        functools.partial(head_kernel, blocks),
        [pltpu.with_memory_space_constraint(x, pltpu.HBM) for x in (snapshots, right_basis)],
        [((rows, cols), f32)] + whole + lefts,
        in_specs=[HBM] * 2,
        scratch=[
            pltpu.VMEM(right_basis.shape, f32),
            pltpu.SemaphoreType.DMA((blocks,)),
            pltpu.SemaphoreType.DMA,
        ],
        name="head",
    )
    level = threshold[None, :]
    for iteration in range(ITERS):
        pieces = sum_tm(list(zip(left[::2], left[1::2])), n_tm)
        first, second, left_top, left_rest = call(
            functools.partial(product_kernel, blocks, [len(x) for x in pieces]),
            (top, rest, *[x for parts in pieces for x in parts]),
            [((first_rows, cols), f32), ((rank // 2 * 3 + SUBLANES - first_rows, cols), f32)] + [((rows, rank), bf16)] * 2,
            name="products",
        )
        sums = sum_rows((first, second), (0, 1), n_rows)
        start, level = call(
            inverse_kernel,
            (sums[0], level),
            [((rank, rank), f32), (level.shape, f32)],
            cost=pl.CostEstimate(flops=80 * rank**3, bytes_accessed=rank * rank * 8, transcendentals=0),
            name="inverse",
        )
        prepared = call(
            prepare_kernel,
            (*sums[:2], start),
            [((rank, rank), bf16)] * 5 + [((rank, 128), f32)],
            cost=pl.CostEstimate(flops=60 * rank**3, bytes_accessed=rank * rank * 8, transcendentals=0),
            name="prepare",
        )
        args = (*sums, *prepared, left_top, left_rest, data, level)
        if iteration < ITERS - 1:
            top, rest, *left = call(
                functools.partial(middle_kernel, blocks),
                args,
                whole + lefts,
                name="middle",
            )
    return call(
        functools.partial(last_kernel, blocks),
        args,
        [((rows, cols), f32)] * 2,
        out_specs=[HBM] * 2,
        scratch=[pltpu.VMEM((rows, cols), f32)] * 2 + [pltpu.SemaphoreType.DMA((2 * blocks,))],
        name="last",
    )


def solution(mesh):
    return jax.shard_map(
        functools.partial(per_device, mesh.shape["tm"], mesh.shape["rows"]),
        mesh=mesh,
        in_specs=(P("rows", "tm"), P("tm", None), P("tm")),
        out_specs=(P("rows", "tm"), P("rows", "tm")),
        check_vma=False,
    )
```
